32 devices in a mesh: chain: 2 (over y), block: 4 (over x, core), shot: 4 (over z).
Axes of the slice: x: 2, y: 2, z: 4, core: 2. Of those that a mesh axis runs over, the one named last changes fastest.
Arguments:
- courant: float32 [64, 64, 256], P('chain', 'block'), parts along dimension 0, may hold values from 0.04 to 0.18
- snapshots: bfloat16 [32, 4, 32, 64, 256], P(('chain', 'shot'), None, None, 'block'), parts along dimension 0, may hold values from -6 to 6
- residuals: float32 [32, 5, 2048], P(('chain', 'shot')), parts along dimension 0, may hold values from -6 to 6
- receivers: int32 [32, 3, 2048], P(('chain', 'shot')), parts along dimension 0, may hold values from 0 to 255, as said below
- sources: int32 [32, 3], P(('chain', 'shot')), parts along dimension 0, may hold values from 0 to 255, as said below
- snap_steps: int32 [32, 4], P(('chain', 'shot')), parts along dimension 0, may hold values from 0 to 3
- live_counts: int32 [8], P(('chain', 'shot')), parts along dimension 0, may hold values from 1 to 4, as said below
- mass_spectrum: float32 [512, 64], P(('chain', 'block')), parts along dimension 0, may hold values from 0.2 to 5
Outputs:
- scaled_gradient: float32 [64, 64, 256], P(('chain', 'shot'), 'block'), parts along dimension 0
The draws below stay inside these ranges and needn't reach their ends.
There are 2 independent parts, one for each index of `chain`. The reference program is written for one: setup_inputs(seed, part) draws one part's arguments, and reference() takes and returns one part's arrays. A program takes and returns all parts, laid end to end along the dimension named above; each array names one. Nothing has to cross between parts.
Inputs may be any that keep to these rules, and one draw needn't show every extreme that they name: `receivers`: each index lies inside the grid (depth below 32, x below 64, y below 256); every coordinate's largest value is reached. `sources`: each index lies inside the grid (depth below 32, x below 64, y below 256); every coordinate's largest value is reached. `live_counts`: slots from the count on hold no live shot; some group is full.
All inputs are finite; a program needn't handle non-finite values.
Results may differ from the reference program's by a relative error of at most 0.0003.
Values sent between devices are 32-bit elements; how exact they have to be, the bound alone decides.
A program may use at most 64 MiB of HBM per device.

```python
import math
import jax
import jax.numpy as jnp
from jax import lax

NY = 256
NZ = 32
SHOTS_DEV = 4
SNAPS = 4
STEPS = 4
RECV = 2048
NX = 64
GROUPS = 4
SHOTS = 16


def draw_receivers(key, part):
    key = jax.random.fold_in(key, 11)
    keys = jax.random.split(key, 3)
    depth_index = jax.random.randint(keys[0], (SHOTS, 1, RECV), 0, NZ)
    across_index = jax.random.randint(keys[1], (SHOTS, 1, RECV), 0, NX)
    lateral_index = jax.random.randint(keys[2], (SHOTS, 1, RECV), 0, NY)
    stacked = jnp.concatenate([depth_index, across_index, lateral_index], axis=1).astype(jnp.int32)
    stacked = stacked.at[0, 0, 0].set(NZ - 1).at[0, 1, 0].set(NX - 1).at[0, 2, 0].set(NY - 1)
    return stacked.at[0, :, 1].set(0)


def draw_sources(key, part):
    key = jax.random.fold_in(key, 23)
    keys = jax.random.split(key, 3)
    depth_index = jax.random.randint(keys[0], (SHOTS, 1), 0, NZ)
    across_index = jax.random.randint(keys[1], (SHOTS, 1), 0, NX)
    lateral_index = jax.random.randint(keys[2], (SHOTS, 1), 0, NY)
    stacked = jnp.concatenate([depth_index, across_index, lateral_index], axis=1).astype(jnp.int32)
    stacked = stacked.at[0, 0].set(NZ - 1).at[0, 1].set(NX - 1).at[0, 2].set(NY - 1)
    return stacked.at[1, :].set(0)


def draw_live_counts(key, part):
    key = jax.random.fold_in(key, 37)
    keys = jax.random.split(key, 2)
    baseline = jax.random.randint(keys[0], (GROUPS,), 1, SHOTS_DEV + 1)
    chosen = jax.random.randint(keys[1], (), 0, GROUPS)
    return baseline.at[chosen].set(SHOTS_DEV).astype(jnp.int32)


def plant(result, own_key, least, high):
    dims = result.shape
    spot = [jax.random.randint(jax.random.fold_in(own_key, axis), (), 0, dims[axis]) for axis in range(len(dims))]
    result = result.at[tuple(spot)].set(least)
    longest = dims.index(max(dims))
    spot[longest] = (spot[longest] + 1) % dims[longest]
    return result.at[tuple(spot)].set(high)


def shard_levels(stream_key, extent, shards, low, top_value):
    loudness, own = 1.0, jax.random.fold_in(stream_key, 6)
    for position, parts in shards:
        draws = jnp.exp(jax.random.uniform(jax.random.fold_in(own, position), (parts,), jnp.float32, low / len(shards), top_value / len(shards)))
        loudness = loudness * jnp.repeat(draws, extent[position] // parts).reshape([-1 if axis == position else 1 for axis in range(len(extent))])
    return loudness


def gaussian(own_key, extent, deviation, most, cuts=(), kind=jnp.bfloat16):
    level = shard_levels(own_key, extent, cuts, -0.22, 0.18) if cuts else 1.0
    entries = jax.random.normal(own_key, extent, jnp.float32) * deviation * level
    return jnp.minimum(jnp.maximum(entries, -most), most).astype(kind)


def setup_inputs(seed: int = 0, part: int = 0) -> dict:
    arg_keys = jax.random.split(jax.random.key(seed), 9)
    part_splits = jax.random.split(jax.random.fold_in(arg_keys[8], part), 9)
    courant = jnp.clip(0.04 + 0.14000001 * jax.random.uniform(part_splits[0], (NZ, NX, NY), jnp.float32) ** shard_levels(part_splits[0], (NZ, NX, NY), ((1, 4),), -0.2, 0.2), 0.04, 0.18)
    snapshots = gaussian(part_splits[1], (SHOTS, SNAPS, NZ, NX, NY), 1.0, 6.0, ((0, 4), (3, 4)))
    residuals = gaussian(part_splits[2], (SHOTS, STEPS + 1, RECV), 1.0, 6.0, ((0, 4),), jnp.float32)
    receivers = draw_receivers(jax.random.fold_in(jax.random.fold_in(arg_keys[8], part), 71), part)
    sources = draw_sources(jax.random.fold_in(jax.random.fold_in(arg_keys[8], part), 71), part)
    snap_steps = plant(jax.random.randint(part_splits[5], (SHOTS, STEPS), 0, SNAPS), jax.random.fold_in(part_splits[5], 1), 0, SNAPS - 1).astype(jnp.int32)
    live_counts = draw_live_counts(jax.random.fold_in(jax.random.fold_in(arg_keys[8], part), 71), part)
    mass_spectrum = jnp.clip(jnp.exp(math.log(5.0) - 3.218876 * jax.random.uniform(part_splits[7], (NY, NX), jnp.float32) ** shard_levels(part_splits[7], (NY, NX), ((0, 4),), -0.2, 0.2)), 0.2, 5.0)
    return {"courant": courant, "snapshots": snapshots, "residuals": residuals, "receivers": receivers, "sources": sources, "snap_steps": snap_steps, "live_counts": live_counts, "mass_spectrum": mass_spectrum}


stencil_weights = (-205.0 / 72.0, 8.0 / 5.0, -1.0 / 5.0, 8.0 / 315.0, -1.0 / 560.0)
mute_radius = 6.0


def laplace_padded(widened):
    lead = [(0, 0)] * (widened.ndim - 3)
    padded = jnp.pad(widened, lead + [(4, 4), (0, 0), (4, 4)])
    depth_cells = widened.shape[-3]
    slab_cells = widened.shape[-2] - 8
    lateral_cells = widened.shape[-1]
    centre = padded[..., 4:4 + depth_cells, 4:4 + slab_cells, 4:4 + lateral_cells]
    accumulated = 3.0 * stencil_weights[0] * centre
    for k in range(1, 5):
        pair = padded[..., 4 + k:4 + k + depth_cells, 4:4 + slab_cells, 4:4 + lateral_cells]
        pair = pair + padded[..., 4 - k:4 - k + depth_cells, 4:4 + slab_cells, 4:4 + lateral_cells]
        pair = pair + padded[..., 4:4 + depth_cells, 4 + k:4 + k + slab_cells, 4:4 + lateral_cells]
        pair = pair + padded[..., 4:4 + depth_cells, 4 - k:4 - k + slab_cells, 4:4 + lateral_cells]
        pair = pair + padded[..., 4:4 + depth_cells, 4:4 + slab_cells, 4 + k:4 + k + lateral_cells]
        pair = pair + padded[..., 4:4 + depth_cells, 4:4 + slab_cells, 4 - k:4 - k + lateral_cells]
        accumulated = accumulated + stencil_weights[k] * pair
    return accumulated


def reference(courant, snapshots, residuals, receivers, sources, snap_steps, live_counts, mass_spectrum):
    depth_cells, across_cells, lateral_cells = courant.shape
    shot_total = snapshots.shape[0]
    slot_count = shot_total // live_counts.shape[0]
    step_count = snap_steps.shape[1]
    depth_pos = jnp.arange(depth_cells).astype(jnp.float32)[:, None, None]
    across_pos = jnp.arange(across_cells).astype(jnp.float32)[None, :, None]
    lateral_pos = jnp.arange(lateral_cells).astype(jnp.float32)[None, None, :]

    def shot_image(shot_index, gradient):
        receiver_set = lax.dynamic_index_in_dim(receivers, shot_index, 0, keepdims=False)
        trace_set = lax.dynamic_index_in_dim(residuals, shot_index, 0, keepdims=False)
        snapshot_set = lax.dynamic_index_in_dim(snapshots, shot_index, 0, keepdims=False)
        step_table = lax.dynamic_index_in_dim(snap_steps, shot_index, 0, keepdims=False)
        source_pos = lax.dynamic_index_in_dim(sources, shot_index, 0, keepdims=False).astype(jnp.float32)

        def inject(t):
            empty = jnp.zeros((depth_cells, across_cells, lateral_cells), jnp.float32)
            return empty.at[receiver_set[0], receiver_set[1], receiver_set[2]].add(trace_set[t])

        previous = jnp.zeros((depth_cells, across_cells, lateral_cells), jnp.float32)
        current = inject(0)
        gradient_part = jnp.zeros((depth_cells, across_cells, lateral_cells), jnp.float32)
        for t in range(1, step_count + 1):
            widened = jnp.pad(current, ((0, 0), (4, 4), (0, 0)))
            advanced = 2.0 * current - previous + courant * laplace_padded(widened) + inject(t)
            chosen = lax.dynamic_index_in_dim(snapshot_set, step_table[t - 1], 0, keepdims=False)
            gradient_part = gradient_part + advanced * chosen.astype(jnp.float32)
            previous, current = current, advanced
        distance = (depth_pos - source_pos[0]) ** 2 + (across_pos - source_pos[1]) ** 2 + (lateral_pos - source_pos[2]) ** 2
        source_mute = 1.0 - jnp.exp(-distance / (mute_radius * mute_radius))
        group_live = lax.dynamic_index_in_dim(live_counts, shot_index // slot_count, 0, keepdims=False)
        live_flag = (shot_index % slot_count < group_live).astype(jnp.float32)
        return gradient + live_flag * (source_mute * gradient_part)

    gradient = lax.fori_loop(jnp.int32(0), jnp.int32(shot_total), shot_image,
                             jnp.zeros((depth_cells, across_cells, lateral_cells), jnp.float32))
    spectrum = jnp.fft.fft2(gradient, axes=(1, 2))
    scaled = jnp.fft.ifft2(spectrum * mass_spectrum.T[None, :, :], axes=(1, 2))
    return jnp.real(scaled).astype(jnp.float32)
```

```python
import functools
import math

import jax
import jax.numpy as jnp
import ml_dtypes
import numpy as np
from jax import lax
from jax.experimental import pallas as pl
from jax.experimental.pallas import tpu as pltpu
from jax.sharding import PartitionSpec as P

stencil_weights = (-205.0 / 72.0, 8.0 / 5.0, -1.0 / 5.0, 8.0 / 315.0, -1.0 / 560.0)
mute_radius = 6.0
MESH = pl.DeviceIdType.MESH
VM = pl.BlockSpec(memory_space=pltpu.VMEM)
SM = pl.BlockSpec(memory_space=pltpu.SMEM)
FULL = lax.Precision.HIGHEST


def two_parts(table):
    table = np.asarray(table, np.float32)
    high = table.astype(ml_dtypes.bfloat16)
    low = (table - high.astype(np.float32)).astype(ml_dtypes.bfloat16)
    return high, low


def difference_table(rows, columns):
    gap = np.abs(np.asarray(rows)[:, None] - np.asarray(columns)[None, :])
    table = np.zeros(gap.shape, np.float64)
    for k in range(1, 5):
        table[gap == k] = stencil_weights[k]
    return table


def across_tables(planes, slab):
    cells = np.arange(slab)
    ghost = np.concatenate([np.arange(-4, 0), np.arange(slab, slab + 4)])
    eye = np.eye(planes)
    return np.concatenate(
        [
            np.kron(eye, difference_table(cells, cells)),
            np.kron(eye, difference_table(cells, ghost)),
        ],
        axis=1,
    )


def fourier_np(length):
    counting = np.arange(length)
    angle = (counting[:, None] * counting[None, :] % length) * (2.0 * math.pi / length)
    return np.cos(angle), np.sin(angle)


def inject_kernel(slab, receivers_ref, residuals_ref, out_ref):
    start = lax.axis_index("block") * slab
    rows = out_ref.shape[2]
    lateral = out_ref.shape[3]
    steps = residuals_ref.shape[1]
    count = receivers_ref.shape[2]
    depth = receivers_ref[0, 0:1, :]
    local = receivers_ref[0, 1:2, :] - start
    side = receivers_ref[0, 2:3, :]
    inside = (local >= 0) & (local < slab)
    place = jnp.where(inside, depth * slab + local, -1)
    row_pick = lax.broadcasted_iota(jnp.int32, (rows, count), 0) == place
    row_pick = jnp.where(row_pick, 1.0, 0.0).astype(jnp.bfloat16)
    side_pick = lax.broadcasted_iota(jnp.int32, (lateral, count), 0) == side
    dims = (((1,), (1,)), ((), ()))
    for t in range(steps):
        value = residuals_ref[0, t : t + 1, :]
        high = value.astype(jnp.bfloat16).astype(jnp.float32)
        low = value - high
        total = lax.dot_general(
            row_pick,
            jnp.where(side_pick, high, 0.0).astype(jnp.bfloat16),
            dims,
            preferred_element_type=jnp.float32,
        )
        total += lax.dot_general(
            row_pick,
            jnp.where(side_pick, low, 0.0).astype(jnp.bfloat16),
            dims,
            preferred_element_type=jnp.float32,
        )
        out_ref[0, t] = total


def inject_all(receivers, residuals, depth_cells, slab, lateral):
    slots, steps, count = residuals.shape
    rows = depth_cells * slab
    return pl.pallas_call(
        functools.partial(inject_kernel, slab),
        grid=(slots,),
        in_specs=[
            pl.BlockSpec((1, 3, count), lambda s: (s, 0, 0)),
            pl.BlockSpec((1, steps, count), lambda s: (s, 0, 0)),
        ],
        out_specs=pl.BlockSpec((1, steps, rows, lateral), lambda s: (s, 0, 0, 0)),
        out_shape=jax.ShapeDtypeStruct((slots, steps, rows, lateral), jnp.float32),
        compiler_params=pltpu.CompilerParams(vmem_limit_bytes=50 * 2**20),
    )(receivers, residuals)


def split_value(value):
    high = value.astype(jnp.bfloat16)
    low = (value - high.astype(jnp.float32)).astype(jnp.bfloat16)
    return high, low


def dot(left, right):
    return jnp.dot(left, right, preferred_element_type=jnp.float32)


def dot_full(left, right):
    return jnp.dot(left, right, preferred_element_type=jnp.float32, precision=FULL)


def step_kernel(
    blocks,
    shots,
    fused,
    steps_ref,
    live_ref,
    courant_ref,
    snaps_ref,
    inj_ref,
    fade_depth_ref,
    fade_flat_ref,
    wx_high_ref,
    wx_low_ref,
    wy_high_ref,
    wy_low_ref,
    *rest,
):
    if fused:
        (mass_ref, spread_ref, ahead_y_ref, back_y_ref, ahead_x_ref, back_x_ref, *rest) = rest
    (out_ref, field, ghost, outgoing, gradient, ghost_send, ghost_recv, *rest) = rest
    slots, step_count = steps_ref.shape
    depth_cells, slab, lateral = courant_ref.shape
    half = depth_cells // 2
    block = lax.axis_index("block")
    shot = lax.axis_index("shot")

    barrier = pltpu.get_barrier_semaphore()

    @pl.when(block > 0)
    def _():
        pl.semaphore_signal(barrier, inc=1, device_id={"block": block - 1}, device_id_type=MESH)

    @pl.when(block < blocks - 1)
    def _():
        pl.semaphore_signal(barrier, inc=1, device_id={"block": block + 1}, device_id_type=MESH)

    if fused:
        (
            mass_all,
            parts,
            total,
            pencil,
            filtered,
            returned,
            mass_sems,
            part_sems,
            pencil_sems,
            return_sems,
        ) = rest
        for off in range(1, blocks):
            peer = lax.rem(block + off, blocks)

            @pl.when((peer != block - 1) & (peer != block + 1))
            def _(peer=peer):
                pl.semaphore_signal(barrier, inc=1, device_id={"block": peer}, device_id_type=MESH)

        for off in range(1, shots):
            peer = lax.rem(shot + off, shots)
            pl.semaphore_signal(barrier, inc=1, device_id={"shot": peer}, device_id_type=MESH)
        pl.semaphore_wait(barrier, blocks - 1 + shots - 1)
    else:

        @pl.when(block > 0)
        def _():
            pl.semaphore_wait(barrier, 1)

        @pl.when(block < blocks - 1)
        def _():
            pl.semaphore_wait(barrier, 1)

    def exchange(sems, axis, size, me, src, dst):
        copies = []
        for off in range(1, size):
            peer = lax.rem(me + off, size)
            copies.append(
                pltpu.make_async_remote_copy(
                    src_ref=src(peer),
                    dst_ref=dst(me),
                    send_sem=sems.at[0, off],
                    recv_sem=sems.at[1, off],
                    device_id={axis: peer},
                    device_id_type=MESH,
                )
            )
        return copies

    if fused:
        mass_copies = exchange(
            mass_sems, "block", blocks, block, lambda p: mass_ref, lambda m: mass_all.at[m]
        )
        for copy in mass_copies:
            copy.start()
        mass_all[block] = mass_ref[...]

    def to_left(t, s):
        return pltpu.make_async_remote_copy(
            src_ref=outgoing.at[t, s, 0],
            dst_ref=ghost.at[t, s, 1],
            send_sem=ghost_send.at[t, s, 0],
            recv_sem=ghost_recv.at[t, s, 1],
            device_id={"block": lax.rem(block + blocks - 1, blocks)},
            device_id_type=MESH,
        )

    def to_right(t, s):
        return pltpu.make_async_remote_copy(
            src_ref=outgoing.at[t, s, 1],
            dst_ref=ghost.at[t, s, 0],
            send_sem=ghost_send.at[t, s, 1],
            recv_sem=ghost_recv.at[t, s, 0],
            device_id={"block": lax.rem(block + 1, blocks)},
            device_id_type=MESH,
        )

    lower = lax.broadcasted_iota(jnp.int32, (half, 8, lateral), 1) < 4

    def swap(value):
        return jnp.concatenate([value[:, 4:8], value[:, 0:4]], axis=1)

    def send_faces(t, s, plane):
        first = field[plane, s, pl.ds(4, half), 0:8, :]
        second = field[plane, s, pl.ds(4 + half, half), 0:8, :]
        outgoing[t, s, 0] = jnp.where(lower, first, swap(second))
        first = field[plane, s, pl.ds(4, half), slab - 8 : slab, :]
        second = field[plane, s, pl.ds(4 + half, half), slab - 8 : slab, :]
        outgoing[t, s, 1] = jnp.where(lower, swap(first), second)

        @pl.when(block > 0)
        def _():
            to_left(t, s).start()

        @pl.when(block < blocks - 1)
        def _():
            to_right(t, s).start()

    def prepare(s, carry):
        edge = jnp.zeros((4, slab, lateral), jnp.float32)
        for plane in range(2):
            field[plane, s, 0:4] = edge
            field[plane, s, depth_cells + 4 : depth_cells + 8] = edge
        field[0, s, 4 : 4 + depth_cells] = inj_ref[s, 0].reshape(depth_cells, slab, lateral)
        field[1, s, 4 : 4 + depth_cells] = jnp.zeros((depth_cells, slab, lateral), jnp.float32)
        send_faces(0, s, 0)
        return carry

    lax.fori_loop(0, slots, prepare, 0)
    gradient[...] = jnp.zeros_like(gradient)

    @pl.when(block == 0)
    def _():
        ghost[:, :, 0] = jnp.zeros((step_count, slots, half, 8, lateral), jnp.float32)

    @pl.when(block == blocks - 1)
    def _():
        ghost[:, :, 1] = jnp.zeros((step_count, slots, half, 8, lateral), jnp.float32)

    def advance(index, carry):
        t = index // slots
        s = lax.rem(index, slots)
        now = lax.rem(t, 2)
        before = 1 - now

        @pl.when(block > 0)
        def _():
            to_right(t, s).wait_recv()

        @pl.when(block < blocks - 1)
        def _():
            to_left(t, s).wait_recv()

        from_left = ghost[t, s, 0]
        from_right = ghost[t, s, 1]
        sides = (
            jnp.where(lower, from_left, swap(from_right)),
            jnp.where(lower, swap(from_left), from_right),
        )
        chosen = steps_ref[s, t]
        live = live_ref[s]
        for c in range(2):
            base = c * half
            centre = field[now, s, 4 + base : 4 + base + half]
            flat = centre.reshape(half * slab, lateral)
            high, low = split_value(flat)
            side_high, side_low = split_value(sides[c].reshape(half * 8, lateral))
            bend = dot(high, wy_high_ref[...])
            bend += dot(low, wy_high_ref[...])
            bend += dot(high, wy_low_ref[...])
            bend += dot(wx_high_ref[...], jnp.concatenate([high, side_high], axis=0))
            bend += dot(wx_high_ref[...], jnp.concatenate([low, side_low], axis=0))
            bend += dot(wx_low_ref[...], jnp.concatenate([high, side_high], axis=0))
            bend = bend.reshape(half, slab, lateral)
            bend += 3.0 * stencil_weights[0] * centre
            for k in range(1, 5):
                up = field[now, s, 4 + base + k : 4 + base + k + half]
                down = field[now, s, 4 + base - k : 4 + base - k + half]
                bend += stencil_weights[k] * (up + down)
            old = field[before, s, 4 + base : 4 + base + half]
            source = inj_ref[s, t + 1, base * slab : (base + half) * slab, :]
            fresh = (
                2.0 * centre
                - old
                + courant_ref[base : base + half] * bend
                + source.reshape(half, slab, lateral)
            )
            field[before, s, 4 + base : 4 + base + half] = fresh
            fade = live - (live * fade_depth_ref[s, base : base + half]) * fade_flat_ref[s][None]
            shown = snaps_ref[s, chosen, base : base + half].astype(jnp.float32)
            gradient[base : base + half] += fade * (fresh * shown)

        @pl.when(t < step_count - 1)
        def _():
            send_faces(t + 1, s, before)

        return carry

    lax.fori_loop(0, step_count * slots, advance, 0)

    def drain(index, carry):
        t = index // slots
        s = lax.rem(index, slots)

        @pl.when(block > 0)
        def _():
            to_left(t, s).wait_send()

        @pl.when(block < blocks - 1)
        def _():
            to_right(t, s).wait_send()

        return carry

    if not fused:
        out_ref[...] = gradient[...]
        lax.fori_loop(0, step_count * slots, drain, 0)
        return

    kept = depth_cells // shots
    owned = kept // blocks
    part_copies = exchange(
        part_sems,
        "shot",
        shots,
        shot,
        lambda p: gradient.at[pl.ds(p * kept, kept)],
        lambda m: parts.at[m],
    )
    for copy in part_copies:
        copy.start()
    lax.fori_loop(0, step_count * slots, drain, 0)
    parts[shot] = gradient[pl.ds(shot * kept, kept)]
    for copy in mass_copies:
        copy.wait()
    wide = mass_all[...].reshape(lateral, mass_all.shape[2])
    scale = lax.dot_general(
        spread_ref[...],
        wide,
        (((1,), (1,)), ((), ())),
        preferred_element_type=jnp.float32,
        precision=FULL,
    )
    for copy in part_copies:
        copy.wait()
    summed = parts[0]
    for i in range(1, shots):
        summed = summed + parts[i]
    total[...] = summed
    pencil_copies = exchange(
        pencil_sems,
        "block",
        blocks,
        block,
        lambda p: total.at[pl.ds(p * owned, owned)],
        lambda m: pencil.at[m],
    )
    for copy in pencil_copies:
        copy.start()
    pencil[block] = total[pl.ds(block * owned, owned)]
    for copy in pencil_copies:
        copy.wait()
    cells = blocks * owned * slab

    def combine(table_ref, pair, sign):
        both = dot_full(table_ref[...], pair)
        real = both[:cells, :lateral] + sign * both[cells:, lateral:]
        imag = both[:cells, lateral:] - sign * both[cells:, :lateral]
        return real, imag

    pair = dot_full(pencil[...].reshape(cells, lateral), ahead_y_ref[...])
    real, imag = combine(ahead_x_ref, pair, 1.0)
    pair = jnp.concatenate([real * scale, imag * scale], axis=1)
    real, imag = combine(back_x_ref, pair, -1.0)
    result = dot_full(jnp.concatenate([real, imag], axis=1), back_y_ref[...])
    filtered[...] = result.reshape(blocks, owned, slab, lateral)
    return_copies = exchange(
        return_sems,
        "block",
        blocks,
        block,
        lambda p: filtered.at[p],
        lambda m: returned.at[m],
    )
    for copy in return_copies:
        copy.start()
    returned[block] = filtered[block]
    for copy in return_copies:
        copy.wait()
    out_ref[...] = returned[...].reshape(kept, slab, lateral)


def run_steps(blocks, shots, fused, operands, out_dims, mass_dims):
    snap_steps, _, courant = operands[:3]
    slots, step_count = snap_steps.shape
    depth_cells, slab, lateral = courant.shape
    half = depth_cells // 2
    dma = pltpu.SemaphoreType.DMA
    scratch = [
        pltpu.VMEM((2, slots, depth_cells + 8, slab, lateral), jnp.float32),
        pltpu.VMEM((step_count, slots, 2, half, 8, lateral), jnp.float32),
        pltpu.VMEM((step_count, slots, 2, half, 8, lateral), jnp.float32),
        pltpu.VMEM((depth_cells, slab, lateral), jnp.float32),
        dma((step_count, slots, 2)),
        dma((step_count, slots, 2)),
    ]
    if fused:
        kept = depth_cells // shots
        owned = kept // blocks
        scratch += [
            pltpu.VMEM((blocks,) + mass_dims, jnp.float32),
            pltpu.VMEM((shots, kept, slab, lateral), jnp.float32),
            pltpu.VMEM((kept, slab, lateral), jnp.float32),
            pltpu.VMEM((blocks, owned, slab, lateral), jnp.float32),
            pltpu.VMEM((blocks, owned, slab, lateral), jnp.float32),
            pltpu.VMEM((blocks, owned, slab, lateral), jnp.float32),
            dma((2, blocks)),
            dma((2, shots)),
            dma((2, blocks)),
            dma((2, blocks)),
        ]
    return pl.pallas_call(
        functools.partial(step_kernel, blocks, shots, fused),
        out_shape=jax.ShapeDtypeStruct(out_dims, jnp.float32),
        in_specs=[SM, SM] + [VM] * (len(operands) - 2),
        out_specs=VM,
        scratch_shapes=scratch,
        compiler_params=pltpu.CompilerParams(
            collective_id=0, has_side_effects=True, vmem_limit_bytes=58 * 2**20
        ),
    )(*operands)


def spectral_tail(gradient, mass_spectrum):
    summed = lax.psum_scatter(gradient, "shot", scatter_dimension=0, tiled=True)
    lateral = summed.shape[2]
    cos_y, sin_y = (jnp.asarray(v, jnp.float32) for v in fourier_np(lateral))
    real = jnp.einsum("zxy,yk->zkx", summed, cos_y, precision=FULL)
    imag = -jnp.einsum("zxy,yk->zkx", summed, sin_y, precision=FULL)
    pencils = lax.all_to_all(
        jnp.stack([real, imag]), "block", split_axis=2, concat_axis=3, tiled=True
    )
    across = pencils.shape[3]
    cos_x, sin_x = (jnp.asarray(v, jnp.float32) for v in fourier_np(across))

    def turn(real, imag, sign):
        first = jnp.einsum("zkx,xa->zka", real, cos_x, precision=FULL)
        first += sign * jnp.einsum("zkx,xa->zka", imag, sin_x, precision=FULL)
        second = jnp.einsum("zkx,xa->zka", imag, cos_x, precision=FULL)
        second -= sign * jnp.einsum("zkx,xa->zka", real, sin_x, precision=FULL)
        return first, second

    real, imag = turn(pencils[0], pencils[1], 1.0)
    real, imag = turn(real * mass_spectrum[None], imag * mass_spectrum[None], -1.0)
    back = lax.all_to_all(
        jnp.stack([real, imag]), "block", split_axis=3, concat_axis=2, tiled=True
    )
    spatial = jnp.einsum("zkx,ky->zxy", back[0], cos_y, precision=FULL)
    spatial -= jnp.einsum("zkx,ky->zxy", back[1], sin_y, precision=FULL)
    return spatial / float(across * lateral)


def per_device(
    courant, snapshots, residuals, receivers, sources, snap_steps, live_counts, mass_spectrum
):
    depth_cells, slab, lateral = courant.shape
    slots = snapshots.shape[0]
    blocks = lax.axis_size("block")
    shots = lax.axis_size("shot")
    half = depth_cells // 2
    kept = depth_cells // shots
    fused = kept % blocks == 0

    injected = inject_all(receivers, residuals, depth_cells, slab, lateral)

    live = (jnp.arange(slots) < live_counts[0]).astype(jnp.float32)
    place = sources.astype(jnp.float32)
    scale = 1.0 / (mute_radius * mute_radius)
    depth_gap = jnp.arange(depth_cells).astype(jnp.float32)[None, :] - place[:, 0:1]
    fade_depth = jnp.broadcast_to(
        jnp.exp(-(depth_gap**2) * scale)[:, :, None, None], (slots, depth_cells, 1, lateral)
    )
    across = lax.axis_index("block") * slab + jnp.arange(slab)
    across_gap = across.astype(jnp.float32)[None, :, None] - place[:, 1][:, None, None]
    side_gap = jnp.arange(lateral).astype(jnp.float32)[None, None, :] - place[:, 2][:, None, None]
    fade_flat = jnp.exp(-(across_gap**2 + side_gap**2) * scale)

    wx_high, wx_low = two_parts(across_tables(half, slab))
    wy_high, wy_low = two_parts(difference_table(np.arange(lateral), np.arange(lateral)))
    operands = [
        snap_steps,
        live,
        courant,
        snapshots,
        injected,
        fade_depth,
        fade_flat,
        jnp.asarray(wx_high),
        jnp.asarray(wx_low),
        jnp.asarray(wy_high),
        jnp.asarray(wy_low),
    ]
    if not fused:
        dims = (depth_cells, slab, lateral)
        return spectral_tail(run_steps(blocks, shots, False, operands, dims, None), mass_spectrum)

    owned = kept // blocks
    wide = blocks * slab
    cos_y, sin_y = fourier_np(lateral)
    cos_x, sin_x = fourier_np(wide)
    cells = owned * wide

    def ordered(table):
        grid = np.zeros((owned, wide, blocks, owned, slab))
        for z in range(owned):
            grid[z, :, :, z, :] = table.reshape(wide, blocks, slab)
        return grid.reshape(cells, cells)

    cos_ahead, sin_ahead = ordered(cos_x), ordered(sin_x)
    lanes = -(-wide // 128) * 128
    spread = np.zeros((owned, wide, lanes))
    for z in range(owned):
        spread[z, :, :wide] = np.eye(wide)
    spread = spread.reshape(cells, lanes) / float(wide * lateral)
    mass = jnp.pad(mass_spectrum, ((0, 0), (0, lanes - wide)))
    tables = [
        spread,
        np.concatenate([cos_y, -sin_y], axis=1),
        np.concatenate([cos_y, -sin_y], axis=0),
        np.concatenate([cos_ahead, sin_ahead], axis=0),
        np.concatenate([cos_ahead.T, sin_ahead.T], axis=0),
    ]
    operands += [mass] + [jnp.asarray(table, jnp.float32) for table in tables]
    return run_steps(blocks, shots, True, operands, (kept, slab, lateral), mass.shape)


def solution(mesh):
    in_specs = (
        P("chain", "block", None),
        P(("chain", "shot"), None, None, "block", None),
        P(("chain", "shot"), None, None),
        P(("chain", "shot"), None, None),
        P(("chain", "shot"), None),
        P(("chain", "shot"), None),
        P(("chain", "shot")),
        P(("chain", "block"), None),
    )
    out_specs = P(("chain", "shot"), "block", None)
    return jax.shard_map(
        per_device, mesh=mesh, in_specs=in_specs, out_specs=out_specs, check_vma=False
    )
```

```python
import functools
import math

import jax
import jax.numpy as jnp
import numpy as np
from jax import lax
from jax.experimental import pallas as pl
from jax.experimental.pallas import tpu as pltpu
from jax.sharding import PartitionSpec as P

stencil_weights = (-205.0 / 72.0, 8.0 / 5.0, -1.0 / 5.0, 8.0 / 315.0, -1.0 / 560.0)
mute_radius = 6.0
MESH = pl.DeviceIdType.MESH
VM = pl.BlockSpec(memory_space=pltpu.VMEM)
SM = pl.BlockSpec(memory_space=pltpu.SMEM)
FULL = lax.Precision.HIGHEST


stencil_unit = 8.0 / 315.0
unit_weights = (None, 63.0, -63.0 / 8.0, 1.0, -9.0 / 128.0)
centre_units = 3.0 * stencil_weights[0] / stencil_unit


def difference_table(rows, columns):
    gap = np.abs(np.asarray(rows)[:, None] - np.asarray(columns)[None, :])
    table = np.zeros(gap.shape, np.float64)
    for k in range(1, 5):
        table[gap == k] = unit_weights[k]
    return table


def plane_tables(planes, slab):
    cells = np.arange(slab)
    ghost = np.concatenate([np.arange(-4, 0), np.arange(slab, slab + 4)])
    depth = np.arange(planes)
    own = np.kron(np.eye(planes), difference_table(cells, cells))
    own += np.kron(difference_table(depth, depth), np.eye(slab))
    sides = np.kron(np.eye(planes), difference_table(cells, ghost))
    tables = []
    for near in (np.arange(planes, planes + 4), np.arange(-4, 0)):
        reach = np.kron(difference_table(depth, near), np.eye(slab))
        spare = np.zeros((planes * slab, 4 * slab))
        one = np.concatenate([own, sides, reach, spare], axis=1)
        tables.append(np.concatenate([one, one], axis=1))
    return np.stack(tables)


def fourier_np(length):
    counting = np.arange(length)
    angle = (counting[:, None] * counting[None, :] % length) * (2.0 * math.pi / length)
    return np.cos(angle), np.sin(angle)


NT = (((1,), (1,)), ((), ()))
GROUP = 128


def inject_kernel(
    slab,
    own_size,
    edge_size,
    receivers_ref,
    residuals_ref,
    sources_ref,
    live_ref,
    tri_ref,
    out_ref,
    ghost_ref,
    fade_ref,
    marks,
    facts,
    ranks,
):
    s = pl.program_id(0)
    start = lax.axis_index("block") * slab
    steps = residuals_ref.shape[0]
    count = receivers_ref.shape[2]
    chunks = count // GROUP
    rows, lateral = out_ref.shape[2:]
    ghost_rows = ghost_ref.shape[1]
    depth_cells = rows // slab

    live = jnp.where(s < live_ref[0], 1.0, 0.0)
    scale = 1.0 / (mute_radius * mute_radius)
    place = [sources_ref[s, i].astype(jnp.float32) for i in range(3)]
    flat = (slab, lateral)
    across = (lax.broadcasted_iota(jnp.int32, flat, 0) + start).astype(jnp.float32) - place[1]
    side = lax.broadcasted_iota(jnp.int32, flat, 1).astype(jnp.float32) - place[2]
    fade_flat = live * jnp.exp(-(across * across + side * side) * scale)
    for z in range(depth_cells):
        gap = jnp.full(flat, z, jnp.float32) - place[0]
        fade_ref[0, z] = live - jnp.exp(-(gap * gap) * scale) * fade_flat

    depth = receivers_ref[0, pl.ds(s, 1), :]
    local = receivers_ref[1, pl.ds(s, 1), :] - start
    lateral_pos = receivers_ref[2, pl.ds(s, 1), :]
    facts[0:1, :] = depth.astype(jnp.float32)
    facts[2:3, :] = (lateral_pos // 16).astype(jnp.float32)
    facts[3:4, :] = lax.rem(lateral_pos, 16).astype(jnp.float32)
    for t in range(steps):
        value = residuals_ref[t, pl.ds(s, 1), :]
        high = value.astype(jnp.bfloat16).astype(jnp.float32)
        facts[4 + 2 * t : 5 + 2 * t, :] = high
        facts[5 + 2 * t : 6 + 2 * t, :] = value - high
    used = 4 + 2 * steps
    facts[used:, :] = jnp.zeros((facts.shape[0] - used, count), jnp.float32)

    def rank(inside):
        flag = jnp.where(inside, 1.0, 0.0)
        for c in range(chunks):
            marks[c : c + 1, :] = flag[:, c * GROUP : (c + 1) * GROUP]
        mark = marks[...]
        through = jnp.dot(
            mark.astype(jnp.bfloat16), tri_ref[...], preferred_element_type=jnp.float32
        )
        total = jnp.zeros((1, 1), jnp.float32)
        for c in range(chunks):
            ranks[c : c + 1, :] = jnp.where(
                mark[c : c + 1] > 0.0, through[c : c + 1] + (total - 1.0), -1.0
            ).astype(jnp.int32)
            total = total + through[c : c + 1, GROUP - 1 :]
        return jnp.sum(flag).astype(jnp.int32)

    def gather(first, size):
        slot = lax.broadcasted_iota(jnp.int32, (size, GROUP), 0) + first
        pick = jnp.concatenate(
            [
                jnp.where(slot == ranks[c : c + 1, :], 1.0, 0.0).astype(jnp.bfloat16)
                for c in range(chunks)
            ],
            axis=1,
        )
        return lax.dot_general(
            facts[...].astype(jnp.bfloat16), pick, NT, preferred_element_type=jnp.float32
        )

    def spread(found, width, row_count, t_list):
        where = found[0:1] * float(width) + found[1:2]
        size = found.shape[1]
        row = lax.broadcasted_iota(jnp.int32, (row_count, size), 0)
        row = jnp.where(row == where.astype(jnp.int32), 1.0, 0.0).astype(jnp.bfloat16)
        row = jnp.concatenate([row, row], axis=1)
        lane = (found[2:3] * 16.0 + found[3:4]).astype(jnp.int32)
        hit = lax.broadcasted_iota(jnp.int32, (lateral, size), 0) == lane
        for t in t_list:
            pair = jnp.concatenate(
                [
                    jnp.where(hit, found[4 + 2 * t + i : 5 + 2 * t + i], 0.0).astype(jnp.bfloat16)
                    for i in range(2)
                ],
                axis=1,
            )
            yield t, lax.dot_general(row, pair, NT, preferred_element_type=jnp.float32)

    inside = (local >= 0) & (local < slab)
    facts[1:2, :] = jnp.where(inside, local, 0).astype(jnp.float32)
    own_total = rank(inside)
    for t, value in spread(gather(0, own_size), slab, rows, range(steps)):
        out_ref[0, t] = value

    def own_group(group, carry):
        for t, add in spread(gather(own_size + group * GROUP, GROUP), slab, rows, range(steps)):
            out_ref[0, t] += add
        return carry

    lax.fori_loop(0, jnp.maximum(own_total - own_size + GROUP - 1, 0) // GROUP, own_group, 0)

    left = (local >= -4) & (local < 0)
    right = (local >= slab) & (local < slab + 4)
    column = jnp.where(left, local + 4, jnp.where(right, local - slab + 4, 0))
    facts[1:2, :] = column.astype(jnp.float32)
    edge_total = rank(left | right)
    for _, value in spread(gather(0, edge_size), 8, ghost_rows, (0,)):
        ghost_ref[0] = value

    def ghost_group(group, carry):
        for _, add in spread(gather(edge_size + group * GROUP, GROUP), 8, ghost_rows, (0,)):
            ghost_ref[0] += add
        return carry

    lax.fori_loop(0, jnp.maximum(edge_total - edge_size + GROUP - 1, 0) // GROUP, ghost_group, 0)


def inject_all(receivers, residuals, sources, live_counts, depth_cells, slab, lateral):
    steps, slots, count = residuals.shape
    rows = depth_cells * slab
    ghost_rows = depth_cells * 8
    blocks = lax.axis_size("block")
    own_size = min(count, (-(-count // blocks // GROUP) + 1) * GROUP)
    edge_size = min(count, (-(-8 * count // (blocks * slab) // GROUP) + 1) * GROUP)
    tri = jnp.asarray(np.triu(np.ones((GROUP, GROUP))), jnp.bfloat16)
    fact_rows = -(-(4 + 2 * steps) // 16) * 16
    return pl.pallas_call(
        functools.partial(inject_kernel, slab, own_size, edge_size),
        grid=(slots,),
        in_specs=[VM, VM, SM, SM, VM],
        out_specs=[
            pl.BlockSpec((1, steps, rows, lateral), lambda s: (s, 0, 0, 0)),
            pl.BlockSpec((1, ghost_rows, lateral), lambda s: (s, 0, 0)),
            pl.BlockSpec((1, depth_cells, slab, lateral), lambda s: (s, 0, 0, 0)),
        ],
        out_shape=[
            jax.ShapeDtypeStruct((slots, steps, rows, lateral), jnp.float32),
            jax.ShapeDtypeStruct((slots, ghost_rows, lateral), jnp.float32),
            jax.ShapeDtypeStruct((slots, depth_cells, slab, lateral), jnp.float32),
        ],
        scratch_shapes=[
            pltpu.VMEM((count // GROUP, GROUP), jnp.float32),
            pltpu.VMEM((fact_rows, count), jnp.float32),
            pltpu.VMEM((count // GROUP, GROUP), jnp.int32),
        ],
        compiler_params=pltpu.CompilerParams(vmem_limit_bytes=62 * 2**20),
    )(receivers, residuals, sources, live_counts, tri)


def split_value(value):
    high = value.astype(jnp.bfloat16)
    low = (value - high.astype(jnp.float32)).astype(jnp.bfloat16)
    return high, low


def dot(left, right):
    return jnp.dot(left, right, preferred_element_type=jnp.float32)


def dot_full(left, right):
    return jnp.dot(left, right, preferred_element_type=jnp.float32, precision=FULL)


def step_kernel(blocks, shots, fused, late, *refs):
    steps_ref, courant_ref, plane_ref, lateral_ref, *rest = refs
    stored = rest[:late]
    if fused:
        mass_ref = rest[late]
        rest = rest[1:]
    out_ref, *rest = rest[late:]
    local = rest[:late]
    (load_sems, field, highs, lows, scaled, gradient, ghost, outgoing, ghost_sems, *rest) = rest[
        late:
    ]
    inj_ref, edge_ref, snaps_ref, fade_ref = local[:4]
    slots, step_count = steps_ref.shape
    depth_cells, slab, lateral = courant_ref.shape
    half = depth_cells // 2
    block = lax.axis_index("block")
    shot = lax.axis_index("shot")

    def load(i, s):
        return pltpu.make_async_copy(stored[i].at[s], local[i].at[s], load_sems.at[i, s])

    def load_table(i):
        return pltpu.make_async_copy(stored[i], local[i], load_sems.at[i, 0])

    for s in range(slots):
        for i in range(4):
            load(i, s).start()
    for i in range(4, late):
        load_table(i).start()

    barrier = pltpu.get_barrier_semaphore()

    @pl.when(block > 0)
    def _():
        pl.semaphore_signal(barrier, inc=1, device_id={"block": block - 1}, device_id_type=MESH)

    @pl.when(block < blocks - 1)
    def _():
        pl.semaphore_signal(barrier, inc=1, device_id={"block": block + 1}, device_id_type=MESH)

    if fused:
        (
            mass_own,
            mass_all,
            parts,
            total,
            pencil,
            filtered,
            returned,
            mass_sems,
            part_sems,
            pencil_sems,
            return_sems,
        ) = rest
        for off in range(1, blocks):
            peer = lax.rem(block + off, blocks)

            @pl.when((peer != block - 1) & (peer != block + 1))
            def _(peer=peer):
                pl.semaphore_signal(barrier, inc=1, device_id={"block": peer}, device_id_type=MESH)

        for off in range(1, shots):
            peer = lax.rem(shot + off, shots)
            pl.semaphore_signal(barrier, inc=1, device_id={"shot": peer}, device_id_type=MESH)
        mass_own[...] = jnp.zeros_like(mass_own)
        mass_own[:, 0 : mass_ref.shape[1]] = mass_ref[...]
    gradient[...] = jnp.zeros_like(gradient)
    scaled[...] = courant_ref[...] * stencil_unit

    @pl.when(block == 0)
    def _():
        ghost[:, :, 0] = jnp.zeros((step_count - 1, slots, half, 8, lateral), jnp.float32)

    @pl.when(block == blocks - 1)
    def _():
        ghost[:, :, 1] = jnp.zeros((step_count - 1, slots, half, 8, lateral), jnp.float32)

    if fused:
        pl.semaphore_wait(barrier, blocks - 1 + shots - 1)
    else:

        @pl.when(block > 0)
        def _():
            pl.semaphore_wait(barrier, 1)

        @pl.when(block < blocks - 1)
        def _():
            pl.semaphore_wait(barrier, 1)

    def exchange(sems, axis, size, me, src, dst):
        copies = []
        for off in range(1, size):
            peer = lax.rem(me + off, size)
            copies.append(
                pltpu.make_async_remote_copy(
                    src_ref=src(peer),
                    dst_ref=dst(me),
                    send_sem=sems.at[0, off],
                    recv_sem=sems.at[1, off],
                    device_id={axis: peer},
                    device_id_type=MESH,
                )
            )
        return copies

    if fused:
        mass_copies = exchange(
            mass_sems, "block", blocks, block, lambda p: mass_own, lambda m: mass_all.at[m]
        )
        for copy in mass_copies:
            copy.start()
        mass_all[block] = mass_own[...]

    def to_left(t, s):
        return pltpu.make_async_remote_copy(
            src_ref=outgoing.at[t, s, 0],
            dst_ref=ghost.at[t, s, 1],
            send_sem=ghost_sems.at[0, t, s, 0],
            recv_sem=ghost_sems.at[1, t, s, 1],
            device_id={"block": lax.rem(block + blocks - 1, blocks)},
            device_id_type=MESH,
        )

    def to_right(t, s):
        return pltpu.make_async_remote_copy(
            src_ref=outgoing.at[t, s, 1],
            dst_ref=ghost.at[t, s, 0],
            send_sem=ghost_sems.at[0, t, s, 1],
            recv_sem=ghost_sems.at[1, t, s, 0],
            device_id={"block": lax.rem(block + 1, blocks)},
            device_id_type=MESH,
        )

    lower = lax.broadcasted_iota(jnp.int32, (half, 8, lateral), 1) < 4

    def swap(value):
        return jnp.concatenate([value[:, 4:8], value[:, 0:4]], axis=1)

    def send_faces(t, s, plane):
        first = field[plane, s, 0:half, 0:8, :]
        second = field[plane, s, half:depth_cells, 0:8, :]
        outgoing[t, s, 0] = jnp.where(lower, first, swap(second))
        first = field[plane, s, 0:half, slab - 8 : slab, :]
        second = field[plane, s, half:depth_cells, slab - 8 : slab, :]
        outgoing[t, s, 1] = jnp.where(lower, swap(first), second)

        @pl.when(block > 0)
        def _():
            to_left(t, s).start()

        @pl.when(block < blocks - 1)
        def _():
            to_right(t, s).start()

    spare = jnp.zeros((4 * slab, lateral), jnp.bfloat16)
    rows = half * slab

    def bend(t, s, c, tile):
        now = t % 2
        near = slice(rows, rows + 4 * slab) if c == 0 else slice(rows - 4 * slab, rows)
        here = slice(c * rows, (c + 1) * rows)
        stack = []
        if t == 0:
            own = split_value(inj_ref[s, 0, here])
            reach = split_value(inj_ref[s, 0, near])
        else:
            own = (highs[now, s, here], lows[now, s, here])
            reach = (highs[now, s, near], lows[now, s, near])
        side = split_value(tile)
        for i in range(2):
            stack += [own[i], side[i], reach[i], spare]
        result = dot(plane_ref[c], jnp.concatenate(stack, axis=0))
        return result + dot(jnp.concatenate(own, axis=1), lateral_ref[...])

    def update(t, s, c, sums):
        now, later = t % 2, (t + 1) % 2
        chosen = steps_ref[s, t]
        for z in range(half):
            depth = c * half + z
            span = slice(depth * slab, (depth + 1) * slab)
            centre = inj_ref[s, 0, span] if t == 0 else field[now, s, depth]
            fresh = 2.0 * centre + inj_ref[s, t + 1, span]
            if t == 1:
                fresh -= inj_ref[s, 0, span]
            elif t > 1:
                fresh -= field[later, s, depth]
            fresh += scaled[depth] * (sums[z * slab : (z + 1) * slab] + centre_units * centre)
            if t < step_count - 1:
                field[later, s, depth] = fresh
                highs[later, s, span], lows[later, s, span] = split_value(fresh)
            shown = snaps_ref[s, chosen, depth].astype(jnp.float32)
            gradient[depth] += fade_ref[s, depth] * (fresh * shown)

    def tiles(t, s):
        if t == 0:
            return [edge_ref[s, c * half * 8 : (c + 1) * half * 8] for c in range(2)]

        from_left = ghost[t - 1, s, 0]
        from_right = ghost[t - 1, s, 1]
        return [
            jnp.where(lower, from_left, swap(from_right)).reshape(half * 8, lateral),
            jnp.where(lower, swap(from_left), from_right).reshape(half * 8, lateral),
        ]

    def arrive(t, s):
        if t == 0:
            for i in (0, 1, 3):
                load(i, s).wait()
            return

        @pl.when(block > 0)
        def _():
            to_right(t - 1, s).wait_recv()

        @pl.when(block < blocks - 1)
        def _():
            to_left(t - 1, s).wait_recv()

    for s in range(slots):
        load(2, s).wait()

    for t in range(step_count - 1):

        def advance(s, carry, t=t):
            arrive(t, s)
            tile = tiles(t, s)
            sums = [bend(t, s, c, tile[c]) for c in range(2)]
            for c in range(2):
                update(t, s, c, sums[c])
            send_faces(t, s, (t + 1) % 2)
            return carry

        lax.fori_loop(0, slots, advance, 0)

    if fused:
        kept = depth_cells // shots
        owned = kept // blocks
        part_copies = exchange(
            part_sems,
            "shot",
            shots,
            shot,
            lambda p: gradient.at[pl.ds(p * kept, kept)],
            lambda m: parts.at[m],
        )
    t = step_count - 1
    for c in range(2):

        def finish(s, carry, c=c):
            if c == 0:
                arrive(t, s)
            update(t, s, c, bend(t, s, c, tiles(t, s)[c]))
            return carry

        lax.fori_loop(0, slots, finish, 0)
        if fused:
            for off in range(1, shots):
                peer = lax.rem(shot + off, shots)

                @pl.when((peer * kept >= c * half) & (peer * kept < (c + 1) * half))
                def _(off=off):
                    part_copies[off - 1].start()

    def drain(index, carry):
        t = index // slots
        s = lax.rem(index, slots)

        @pl.when(block > 0)
        def _():
            to_left(t, s).wait_send()

        @pl.when(block < blocks - 1)
        def _():
            to_right(t, s).wait_send()

        return carry

    lax.fori_loop(0, (step_count - 1) * slots, drain, 0)
    if not fused:
        out_ref[...] = gradient[...]
        return

    for i in range(4, late):
        load_table(i).wait()
    spread_ref, ahead_y_ref, back_y_ref, ahead_x_ref, back_x_ref = local[4:]
    parts[shot] = gradient[pl.ds(shot * kept, kept)]
    for copy in mass_copies:
        copy.wait()
    wide = mass_all[...].reshape(lateral, mass_all.shape[2])
    scale = lax.dot_general(
        spread_ref[...], wide, NT, preferred_element_type=jnp.float32, precision=FULL
    )
    for copy in part_copies:
        copy.wait()
    summed = parts[0]
    for i in range(1, shots):
        summed = summed + parts[i]
    total[...] = summed
    pencil_copies = exchange(
        pencil_sems,
        "block",
        blocks,
        block,
        lambda p: total.at[pl.ds(p * owned, owned)],
        lambda m: pencil.at[m],
    )
    for copy in pencil_copies:
        copy.start()
    pencil[block] = total[pl.ds(block * owned, owned)]
    for copy in pencil_copies:
        copy.wait()
    cells = blocks * owned * slab

    def combine(table_ref, pair, sign):
        both = dot_full(table_ref[...], pair)
        real = both[:cells, :lateral] + sign * both[cells:, lateral:]
        imag = both[:cells, lateral:] - sign * both[cells:, :lateral]
        return real, imag

    pair = dot_full(pencil[...].reshape(cells, lateral), ahead_y_ref[...])
    real, imag = combine(ahead_x_ref, pair, 1.0)
    pair = jnp.concatenate([real * scale, imag * scale], axis=1)
    real, imag = combine(back_x_ref, pair, -1.0)
    result = dot_full(jnp.concatenate([real, imag], axis=1), back_y_ref[...])
    filtered[...] = result.reshape(blocks, owned, slab, lateral)
    return_copies = exchange(
        return_sems,
        "block",
        blocks,
        block,
        lambda p: filtered.at[p],
        lambda m: returned.at[m],
    )
    for copy in return_copies:
        copy.start()
    returned[block] = filtered[block]
    for copy in return_copies:
        copy.wait()
    out_ref[...] = returned[...].reshape(kept, slab, lateral)


def run_steps(blocks, shots, fused, direct, stored, mass, out_dims):
    snap_steps, courant = direct[:2]
    slots, step_count = snap_steps.shape
    depth_cells, slab, lateral = courant.shape
    half = depth_cells // 2
    dma = pltpu.SemaphoreType.DMA
    cube = (depth_cells, slab, lateral)
    scratch = [pltpu.VMEM(array.shape, array.dtype) for array in stored]
    scratch += [
        dma((len(stored), slots)),
        pltpu.VMEM((2, slots) + cube, jnp.float32),
        pltpu.VMEM((2, slots, depth_cells * slab, lateral), jnp.bfloat16),
        pltpu.VMEM((2, slots, depth_cells * slab, lateral), jnp.bfloat16),
        pltpu.VMEM(cube, jnp.float32),
        pltpu.VMEM(cube, jnp.float32),
        pltpu.VMEM((step_count - 1, slots, 2, half, 8, lateral), jnp.float32),
        pltpu.VMEM((step_count - 1, slots, 2, half, 8, lateral), jnp.float32),
        dma((2, step_count - 1, slots, 2)),
    ]
    operands = list(direct) + list(stored)
    specs = [SM] + [VM] * (len(direct) - 1) + [pl.BlockSpec(memory_space=pltpu.HBM)] * len(stored)
    if fused:
        operands.append(mass)
        specs.append(VM)
        kept = depth_cells // shots
        owned = kept // blocks
        lanes = stored[4].shape[1]
        scratch += [
            pltpu.VMEM((mass.shape[0], lanes), jnp.float32),
            pltpu.VMEM((blocks, mass.shape[0], lanes), jnp.float32),
            pltpu.VMEM((shots, kept, slab, lateral), jnp.float32),
            pltpu.VMEM((kept, slab, lateral), jnp.float32),
            pltpu.VMEM((blocks, owned, slab, lateral), jnp.float32),
            pltpu.VMEM((blocks, owned, slab, lateral), jnp.float32),
            pltpu.VMEM((blocks, owned, slab, lateral), jnp.float32),
            dma((2, blocks)),
            dma((2, shots)),
            dma((2, blocks)),
            dma((2, blocks)),
        ]
    return pl.pallas_call(
        functools.partial(step_kernel, blocks, shots, fused, len(stored)),
        out_shape=jax.ShapeDtypeStruct(out_dims, jnp.float32),
        in_specs=specs,
        out_specs=VM,
        scratch_shapes=scratch,
        compiler_params=pltpu.CompilerParams(
            collective_id=0, has_side_effects=True, vmem_limit_bytes=58 * 2**20
        ),
    )(*operands)


def spectral_tail(gradient, mass_spectrum):
    summed = lax.psum_scatter(gradient, "shot", scatter_dimension=0, tiled=True)
    lateral = summed.shape[2]
    cos_y, sin_y = (jnp.asarray(v, jnp.float32) for v in fourier_np(lateral))
    real = jnp.einsum("zxy,yk->zkx", summed, cos_y, precision=FULL)
    imag = -jnp.einsum("zxy,yk->zkx", summed, sin_y, precision=FULL)
    pencils = lax.all_to_all(
        jnp.stack([real, imag]), "block", split_axis=2, concat_axis=3, tiled=True
    )
    across = pencils.shape[3]
    cos_x, sin_x = (jnp.asarray(v, jnp.float32) for v in fourier_np(across))

    def turn(real, imag, sign):
        first = jnp.einsum("zkx,xa->zka", real, cos_x, precision=FULL)
        first += sign * jnp.einsum("zkx,xa->zka", imag, sin_x, precision=FULL)
        second = jnp.einsum("zkx,xa->zka", imag, cos_x, precision=FULL)
        second -= sign * jnp.einsum("zkx,xa->zka", real, sin_x, precision=FULL)
        return first, second

    real, imag = turn(pencils[0], pencils[1], 1.0)
    real, imag = turn(real * mass_spectrum[None], imag * mass_spectrum[None], -1.0)
    back = lax.all_to_all(
        jnp.stack([real, imag]), "block", split_axis=3, concat_axis=2, tiled=True
    )
    spatial = jnp.einsum("zkx,ky->zxy", back[0], cos_y, precision=FULL)
    spatial -= jnp.einsum("zkx,ky->zxy", back[1], sin_y, precision=FULL)
    return spatial / float(across * lateral)


def per_device(
    courant, snapshots, residuals, receivers, sources, snap_steps, live_counts, mass_spectrum
):
    depth_cells, slab, lateral = courant.shape
    blocks = lax.axis_size("block")
    shots = lax.axis_size("shot")
    half = depth_cells // 2
    kept = depth_cells // shots
    fused = kept % blocks == 0

    injected, edges, fade = inject_all(
        jnp.transpose(receivers, (1, 0, 2)),
        jnp.transpose(residuals, (1, 0, 2)),
        sources,
        live_counts,
        depth_cells,
        slab,
        lateral,
    )
    lateral_table = difference_table(np.arange(lateral), np.arange(lateral))
    direct = [
        snap_steps,
        courant,
        jnp.asarray(plane_tables(half, slab), jnp.bfloat16),
        jnp.asarray(np.concatenate([lateral_table] * 2, axis=0), jnp.bfloat16),
    ]
    stored = [injected, edges, snapshots, fade]
    if not fused:
        dims = (depth_cells, slab, lateral)
        summed = run_steps(blocks, shots, False, direct, stored, None, dims)
        return spectral_tail(summed, mass_spectrum)

    owned = kept // blocks
    wide = blocks * slab
    cos_y, sin_y = fourier_np(lateral)
    cos_x, sin_x = fourier_np(wide)
    cells = owned * wide

    def ordered(table):
        grid = np.zeros((owned, wide, blocks, owned, slab))
        for z in range(owned):
            grid[z, :, :, z, :] = table.reshape(wide, blocks, slab)
        return grid.reshape(cells, cells)

    cos_ahead, sin_ahead = ordered(cos_x), ordered(sin_x)
    lanes = -(-wide // 128) * 128
    spread = np.zeros((owned, wide, lanes))
    for z in range(owned):
        spread[z, :, :wide] = np.eye(wide)
    spread = spread.reshape(cells, lanes) / float(wide * lateral)
    tables = [
        spread,
        np.concatenate([cos_y, -sin_y], axis=1),
        np.concatenate([cos_y, -sin_y], axis=0),
        np.concatenate([cos_ahead, sin_ahead], axis=0),
        np.concatenate([cos_ahead.T, sin_ahead.T], axis=0),
    ]
    stored += [jnp.asarray(table, jnp.float32) for table in tables]
    return run_steps(
        blocks, shots, True, direct, stored, mass_spectrum, (kept, slab, lateral)
    )


def solution(mesh):
    in_specs = (
        P("chain", "block", None),
        P(("chain", "shot"), None, None, "block", None),
        P(("chain", "shot"), None, None),
        P(("chain", "shot"), None, None),
        P(("chain", "shot"), None),
        P(("chain", "shot"), None),
        P(("chain", "shot")),
        P(("chain", "block"), None),
    )
    out_specs = P(("chain", "shot"), "block", None)
    return jax.shard_map(
        per_device, mesh=mesh, in_specs=in_specs, out_specs=out_specs, check_vma=False
    )
```

```python
import functools
import math

import jax
import jax.numpy as jnp
import ml_dtypes
import numpy as np
from jax import lax
from jax.experimental import pallas as pl
from jax.experimental.pallas import tpu as pltpu
from jax.sharding import PartitionSpec as P

stencil_weights = (-205.0 / 72.0, 8.0 / 5.0, -1.0 / 5.0, 8.0 / 315.0, -1.0 / 560.0)
mute_radius = 6.0
MESH = pl.DeviceIdType.MESH
VM = pl.BlockSpec(memory_space=pltpu.VMEM)
SM = pl.BlockSpec(memory_space=pltpu.SMEM)
FULL = lax.Precision.HIGHEST


def two_parts(table):
    high = table.astype(ml_dtypes.bfloat16)
    return np.stack([high, (table - high.astype(np.float64)).astype(ml_dtypes.bfloat16)])


stencil_unit = 8.0 / 315.0
unit_weights = (None, 63.0, -63.0 / 8.0, 1.0, -9.0 / 128.0)
centre_units = 3.0 * stencil_weights[0] / stencil_unit


def difference_table(rows, columns):
    gap = np.abs(np.asarray(rows)[:, None] - np.asarray(columns)[None, :])
    table = np.zeros(gap.shape, np.float64)
    for k in range(1, 5):
        table[gap == k] = unit_weights[k]
    return table


def plane_tables(planes, slab):
    cells = np.arange(slab)
    ghost = np.concatenate([np.arange(-4, 0), np.arange(slab, slab + 4)])
    depth = np.arange(planes)
    own = np.kron(np.eye(planes), difference_table(cells, cells))
    own += np.kron(difference_table(depth, depth), np.eye(slab))
    sides = np.kron(np.eye(planes), difference_table(cells, ghost))
    tables = []
    for near in (np.arange(planes, planes + 4), np.arange(-4, 0)):
        reach = np.kron(difference_table(depth, near), np.eye(slab))
        spare = np.zeros((planes * slab, 4 * slab))
        one = np.concatenate([own, sides, reach, spare], axis=1)
        tables.append(np.concatenate([one, one], axis=1))
    return np.stack(tables)


def fourier_np(length):
    counting = np.arange(length)
    angle = (counting[:, None] * counting[None, :] % length) * (2.0 * math.pi / length)
    return np.cos(angle), np.sin(angle)


NT = (((1,), (1,)), ((), ()))
GROUP = 128


def inject_kernel(
    slab,
    own_size,
    edge_size,
    receivers_ref,
    residuals_ref,
    sources_ref,
    live_ref,
    tri_ref,
    out_ref,
    ghost_ref,
    fade_ref,
    marks,
    facts,
    ranks,
):
    s = pl.program_id(0)
    start = lax.axis_index("block") * slab
    steps = residuals_ref.shape[0]
    count = receivers_ref.shape[2]
    chunks = count // GROUP
    rows, lateral = out_ref.shape[2:]
    ghost_rows = ghost_ref.shape[1]
    depth_cells = rows // slab

    live = jnp.where(s < live_ref[0], 1.0, 0.0)
    scale = 1.0 / (mute_radius * mute_radius)
    place = [sources_ref[s, i].astype(jnp.float32) for i in range(3)]
    flat = (slab, lateral)
    across = (lax.broadcasted_iota(jnp.int32, flat, 0) + start).astype(jnp.float32) - place[1]
    side = lax.broadcasted_iota(jnp.int32, flat, 1).astype(jnp.float32) - place[2]
    fade_flat = live * jnp.exp(-(across * across + side * side) * scale)
    for z in range(depth_cells):
        gap = jnp.full(flat, z, jnp.float32) - place[0]
        fade_ref[0, z] = live - jnp.exp(-(gap * gap) * scale) * fade_flat

    depth = receivers_ref[0, pl.ds(s, 1), :]
    local = receivers_ref[1, pl.ds(s, 1), :] - start
    lateral_pos = receivers_ref[2, pl.ds(s, 1), :]
    facts[0:1, :] = depth.astype(jnp.float32)
    facts[2:3, :] = (lateral_pos // 16).astype(jnp.float32)
    facts[3:4, :] = lax.rem(lateral_pos, 16).astype(jnp.float32)
    for t in range(steps):
        value = residuals_ref[t, pl.ds(s, 1), :]
        high = value.astype(jnp.bfloat16).astype(jnp.float32)
        facts[4 + 2 * t : 5 + 2 * t, :] = high
        facts[5 + 2 * t : 6 + 2 * t, :] = value - high
    used = 4 + 2 * steps
    facts[used:, :] = jnp.zeros((facts.shape[0] - used, count), jnp.float32)

    def rank(inside):
        flag = jnp.where(inside, 1.0, 0.0)
        for c in range(chunks):
            marks[c : c + 1, :] = flag[:, c * GROUP : (c + 1) * GROUP]
        mark = marks[...]
        through = jnp.dot(
            mark.astype(jnp.bfloat16), tri_ref[...], preferred_element_type=jnp.float32
        )
        total = jnp.zeros((1, 1), jnp.float32)
        for c in range(chunks):
            ranks[c : c + 1, :] = jnp.where(
                mark[c : c + 1] > 0.0, through[c : c + 1] + (total - 1.0), -1.0
            ).astype(jnp.int32)
            total = total + through[c : c + 1, GROUP - 1 :]
        return jnp.sum(flag).astype(jnp.int32)

    def gather(first, size):
        slot = lax.broadcasted_iota(jnp.int32, (size, GROUP), 0) + first
        pick = jnp.concatenate(
            [
                jnp.where(slot == ranks[c : c + 1, :], 1.0, 0.0).astype(jnp.bfloat16)
                for c in range(chunks)
            ],
            axis=1,
        )
        return lax.dot_general(
            facts[...].astype(jnp.bfloat16), pick, NT, preferred_element_type=jnp.float32
        )

    def spread(found, width, row_count, t_list):
        where = found[0:1] * float(width) + found[1:2]
        size = found.shape[1]
        row = lax.broadcasted_iota(jnp.int32, (row_count, size), 0)
        row = jnp.where(row == where.astype(jnp.int32), 1.0, 0.0).astype(jnp.bfloat16)
        row = jnp.concatenate([row, row], axis=1)
        lane = (found[2:3] * 16.0 + found[3:4]).astype(jnp.int32)
        hit = lax.broadcasted_iota(jnp.int32, (lateral, size), 0) == lane
        for t in t_list:
            pair = jnp.concatenate(
                [
                    jnp.where(hit, found[4 + 2 * t + i : 5 + 2 * t + i], 0.0).astype(jnp.bfloat16)
                    for i in range(2)
                ],
                axis=1,
            )
            yield t, lax.dot_general(row, pair, NT, preferred_element_type=jnp.float32)

    inside = (local >= 0) & (local < slab)
    facts[1:2, :] = jnp.where(inside, local, 0).astype(jnp.float32)
    own_total = rank(inside)
    for t, value in spread(gather(0, own_size), slab, rows, range(steps)):
        out_ref[0, t] = value

    def own_group(group, carry):
        for t, add in spread(gather(own_size + group * GROUP, GROUP), slab, rows, range(steps)):
            out_ref[0, t] += add
        return carry

    lax.fori_loop(0, jnp.maximum(own_total - own_size + GROUP - 1, 0) // GROUP, own_group, 0)

    left = (local >= -4) & (local < 0)
    right = (local >= slab) & (local < slab + 4)
    column = jnp.where(left, local + 4, jnp.where(right, local - slab + 4, 0))
    facts[1:2, :] = column.astype(jnp.float32)
    edge_total = rank(left | right)
    for _, value in spread(gather(0, edge_size), 8, ghost_rows, (0,)):
        ghost_ref[0] = value

    def ghost_group(group, carry):
        for _, add in spread(gather(edge_size + group * GROUP, GROUP), 8, ghost_rows, (0,)):
            ghost_ref[0] += add
        return carry

    lax.fori_loop(0, jnp.maximum(edge_total - edge_size + GROUP - 1, 0) // GROUP, ghost_group, 0)


def inject_all(receivers, residuals, sources, live_counts, depth_cells, slab, lateral):
    steps, slots, count = residuals.shape
    rows = depth_cells * slab
    ghost_rows = depth_cells * 8
    blocks = lax.axis_size("block")
    own_size = min(count, (-(-count // blocks // GROUP) + 1) * GROUP)
    edge_size = min(count, (-(-8 * count // (blocks * slab) // GROUP) + 1) * GROUP)
    tri = jnp.asarray(np.triu(np.ones((GROUP, GROUP))), jnp.bfloat16)
    fact_rows = -(-(4 + 2 * steps) // 16) * 16
    return pl.pallas_call(
        functools.partial(inject_kernel, slab, own_size, edge_size),
        grid=(slots,),
        in_specs=[VM, VM, SM, SM, VM],
        out_specs=[
            pl.BlockSpec((1, steps, rows, lateral), lambda s: (s, 0, 0, 0)),
            pl.BlockSpec((1, ghost_rows, lateral), lambda s: (s, 0, 0)),
            pl.BlockSpec((1, depth_cells, slab, lateral), lambda s: (s, 0, 0, 0)),
        ],
        out_shape=[
            jax.ShapeDtypeStruct((slots, steps, rows, lateral), jnp.float32),
            jax.ShapeDtypeStruct((slots, ghost_rows, lateral), jnp.float32),
            jax.ShapeDtypeStruct((slots, depth_cells, slab, lateral), jnp.float32),
        ],
        scratch_shapes=[
            pltpu.VMEM((count // GROUP, GROUP), jnp.float32),
            pltpu.VMEM((fact_rows, count), jnp.float32),
            pltpu.VMEM((count // GROUP, GROUP), jnp.int32),
        ],
        compiler_params=pltpu.CompilerParams(vmem_limit_bytes=62 * 2**20),
    )(receivers, residuals, sources, live_counts, tri)


def split_value(value):
    high = value.astype(jnp.bfloat16)
    low = (value - high.astype(jnp.float32)).astype(jnp.bfloat16)
    return high, low


def dot(left, right):
    return jnp.dot(left, right, preferred_element_type=jnp.float32)


def dot_right(value, table_ref):
    high, low = split_value(value)
    return dot(high, table_ref[0]) + (dot(low, table_ref[0]) + dot(high, table_ref[1]))


def dot_left(table_ref, value):
    high, low = split_value(value)
    return dot(table_ref[0], high) + (dot(table_ref[0], low) + dot(table_ref[1], high))


def step_kernel(blocks, shots, fused, late, *refs):
    steps_ref, courant_ref, plane_ref, lateral_ref, *rest = refs
    stored = rest[:late]
    if fused:
        mass_ref = rest[late]
        rest = rest[1:]
    out_ref, *rest = rest[late:]
    local = rest[:late]
    (load_sems, field, highs, lows, scaled, gradient, ghost, outgoing, ghost_sems, *rest) = rest[
        late:
    ]
    inj_ref, edge_ref, snaps_ref, fade_ref = local[:4]
    slots, step_count = steps_ref.shape
    depth_cells, slab, lateral = courant_ref.shape
    half = depth_cells // 2
    block = lax.axis_index("block")
    shot = lax.axis_index("shot")

    def load(i, s):
        if i == 0:
            span = (s, slice(0, 2))
            return pltpu.make_async_copy(stored[0].at[span], local[0].at[span], load_sems.at[0, s])
        return pltpu.make_async_copy(stored[i].at[s], local[i].at[s], load_sems.at[i, s])

    def load_later(s):
        span = (s, slice(2, steps_ref.shape[1] + 1))
        return pltpu.make_async_copy(stored[0].at[span], local[0].at[span], load_sems.at[late, s])

    def load_table(i):
        return pltpu.make_async_copy(stored[i], local[i], load_sems.at[i, 0])

    for s in range(slots):
        load(2, s).start()
    for s in range(slots):
        for i in (0, 1, 3):
            load(i, s).start()
    for s in range(slots):
        load_later(s).start()
    for i in range(4, late):
        load_table(i).start()

    barrier = pltpu.get_barrier_semaphore()

    @pl.when(block > 0)
    def _():
        pl.semaphore_signal(barrier, inc=1, device_id={"block": block - 1}, device_id_type=MESH)

    @pl.when(block < blocks - 1)
    def _():
        pl.semaphore_signal(barrier, inc=1, device_id={"block": block + 1}, device_id_type=MESH)

    if fused:
        (
            mass_own,
            mass_all,
            parts,
            total,
            pencil,
            filtered,
            returned,
            mass_sems,
            part_sems,
            pencil_sems,
            return_sems,
        ) = rest
        for off in range(1, blocks):
            peer = lax.rem(block + off, blocks)

            @pl.when((peer != block - 1) & (peer != block + 1))
            def _(peer=peer):
                pl.semaphore_signal(barrier, inc=1, device_id={"block": peer}, device_id_type=MESH)

        for off in range(1, shots):
            peer = lax.rem(shot + off, shots)
            pl.semaphore_signal(barrier, inc=1, device_id={"shot": peer}, device_id_type=MESH)
        mass_own[...] = jnp.zeros_like(mass_own)
        mass_own[:, 0 : mass_ref.shape[1]] = mass_ref[...]
    gradient[...] = jnp.zeros_like(gradient)
    scaled[...] = courant_ref[...] * stencil_unit

    @pl.when(block == 0)
    def _():
        ghost[:, :, 0] = jnp.zeros((step_count - 1, slots, half, 8, lateral), jnp.float32)

    @pl.when(block == blocks - 1)
    def _():
        ghost[:, :, 1] = jnp.zeros((step_count - 1, slots, half, 8, lateral), jnp.float32)

    if fused:
        pl.semaphore_wait(barrier, blocks - 1 + shots - 1)
    else:

        @pl.when(block > 0)
        def _():
            pl.semaphore_wait(barrier, 1)

        @pl.when(block < blocks - 1)
        def _():
            pl.semaphore_wait(barrier, 1)

    def exchange(sems, axis, size, me, src, dst):
        copies = []
        for off in range(1, size):
            peer = lax.rem(me + off, size)
            copies.append(
                pltpu.make_async_remote_copy(
                    src_ref=src(peer),
                    dst_ref=dst(me),
                    send_sem=sems.at[0, off],
                    recv_sem=sems.at[1, off],
                    device_id={axis: peer},
                    device_id_type=MESH,
                )
            )
        return copies

    if fused:
        mass_copies = exchange(
            mass_sems, "block", blocks, block, lambda p: mass_own, lambda m: mass_all.at[m]
        )
        for copy in mass_copies:
            copy.start()
        mass_all[block] = mass_own[...]

    def to_left(t, s):
        return pltpu.make_async_remote_copy(
            src_ref=outgoing.at[t, s, 0],
            dst_ref=ghost.at[t, s, 1],
            send_sem=ghost_sems.at[0, t, s, 0],
            recv_sem=ghost_sems.at[1, t, s, 1],
            device_id={"block": lax.rem(block + blocks - 1, blocks)},
            device_id_type=MESH,
        )

    def to_right(t, s):
        return pltpu.make_async_remote_copy(
            src_ref=outgoing.at[t, s, 1],
            dst_ref=ghost.at[t, s, 0],
            send_sem=ghost_sems.at[0, t, s, 1],
            recv_sem=ghost_sems.at[1, t, s, 0],
            device_id={"block": lax.rem(block + 1, blocks)},
            device_id_type=MESH,
        )

    lower = lax.broadcasted_iota(jnp.int32, (half, 8, lateral), 1) < 4

    def swap(value):
        return jnp.concatenate([value[:, 4:8], value[:, 0:4]], axis=1)

    def send_faces(t, s, plane):
        first = field[plane, s, 0:half, 0:8, :]
        second = field[plane, s, half:depth_cells, 0:8, :]
        outgoing[t, s, 0] = jnp.where(lower, first, swap(second))
        first = field[plane, s, 0:half, slab - 8 : slab, :]
        second = field[plane, s, half:depth_cells, slab - 8 : slab, :]
        outgoing[t, s, 1] = jnp.where(lower, swap(first), second)

        @pl.when(block > 0)
        def _():
            to_left(t, s).start()

        @pl.when(block < blocks - 1)
        def _():
            to_right(t, s).start()

    spare = jnp.zeros((4 * slab, lateral), jnp.bfloat16)
    rows = half * slab

    def bend(t, s, c, tile):
        now = t % 2
        near = slice(rows, rows + 4 * slab) if c == 0 else slice(rows - 4 * slab, rows)
        here = slice(c * rows, (c + 1) * rows)
        stack = []
        if t == 0:
            own = split_value(inj_ref[s, 0, here])
            reach = split_value(inj_ref[s, 0, near])
        else:
            own = (highs[now, s, here], lows[now, s, here])
            reach = (highs[now, s, near], lows[now, s, near])
        side = split_value(tile)
        for i in range(2):
            stack += [own[i], side[i], reach[i], spare]
        result = dot(plane_ref[c], jnp.concatenate(stack, axis=0))
        return result + dot(jnp.concatenate(own, axis=1), lateral_ref[...])

    def update(t, s, c, sums):
        now, later = t % 2, (t + 1) % 2
        chosen = steps_ref[s, t]
        for z in range(half):
            depth = c * half + z
            span = slice(depth * slab, (depth + 1) * slab)
            centre = inj_ref[s, 0, span] if t == 0 else field[now, s, depth]
            fresh = 2.0 * centre + inj_ref[s, t + 1, span]
            if t == 1:
                fresh -= inj_ref[s, 0, span]
            elif t > 1:
                fresh -= field[later, s, depth]
            fresh += scaled[depth] * (sums[z * slab : (z + 1) * slab] + centre_units * centre)
            if t < step_count - 1:
                field[later, s, depth] = fresh
                highs[later, s, span], lows[later, s, span] = split_value(fresh)
            shown = snaps_ref[s, chosen, depth].astype(jnp.float32)
            gradient[depth] += fade_ref[s, depth] * (fresh * shown)

    def tiles(t, s):
        if t == 0:
            return [edge_ref[s, c * half * 8 : (c + 1) * half * 8] for c in range(2)]

        from_left = ghost[t - 1, s, 0]
        from_right = ghost[t - 1, s, 1]
        return [
            jnp.where(lower, from_left, swap(from_right)).reshape(half * 8, lateral),
            jnp.where(lower, swap(from_left), from_right).reshape(half * 8, lateral),
        ]

    def arrive(t, s):
        if t == 0:
            for i in (0, 1, 3):
                load(i, s).wait()
            return
        if t == 1:
            load_later(s).wait()

        @pl.when(block > 0)
        def _():
            to_right(t - 1, s).wait_recv()

        @pl.when(block < blocks - 1)
        def _():
            to_left(t - 1, s).wait_recv()

    for s in range(slots):
        load(2, s).wait()

    for t in range(step_count - 1):

        def advance(s, carry, t=t):
            arrive(t, s)
            tile = tiles(t, s)
            sums = [bend(t, s, c, tile[c]) for c in range(2)]
            for c in range(2):
                update(t, s, c, sums[c])
            send_faces(t, s, (t + 1) % 2)
            return carry

        lax.fori_loop(0, slots, advance, 0)

    if fused:
        kept = depth_cells // shots
        owned = kept // blocks
        part_copies = exchange(
            part_sems,
            "shot",
            shots,
            shot,
            lambda p: gradient.at[pl.ds(p * kept, kept)],
            lambda m: parts.at[m],
        )
    t = step_count - 1
    for c in range(2):

        def finish(s, carry, c=c):
            if c == 0:
                arrive(t, s)
            update(t, s, c, bend(t, s, c, tiles(t, s)[c]))
            return carry

        lax.fori_loop(0, slots, finish, 0)
        if fused:
            for off in range(1, shots):
                peer = lax.rem(shot + off, shots)

                @pl.when((peer * kept >= c * half) & (peer * kept < (c + 1) * half))
                def _(off=off):
                    part_copies[off - 1].start()

    def drain(index, carry):
        t = index // slots
        s = lax.rem(index, slots)

        @pl.when(block > 0)
        def _():
            to_left(t, s).wait_send()

        @pl.when(block < blocks - 1)
        def _():
            to_right(t, s).wait_send()

        return carry

    lax.fori_loop(0, (step_count - 1) * slots, drain, 0)
    if not fused:
        out_ref[...] = gradient[...]
        return

    for i in range(4, late):
        load_table(i).wait()
    spread_ref, ahead_y_ref, back_y_ref, ahead_x_ref, back_x_ref = local[4:]
    parts[shot] = gradient[pl.ds(shot * kept, kept)]
    for copy in mass_copies:
        copy.wait()
    wide = mass_all[...].reshape(lateral, mass_all.shape[2])
    scale = lax.dot_general(
        spread_ref[...], wide, NT, preferred_element_type=jnp.float32, precision=FULL
    )
    for copy in part_copies:
        copy.wait()
    summed = parts[0]
    for i in range(1, shots):
        summed = summed + parts[i]
    total[...] = summed
    pencil_copies = exchange(
        pencil_sems,
        "block",
        blocks,
        block,
        lambda p: total.at[pl.ds(p * owned, owned)],
        lambda m: pencil.at[m],
    )
    for copy in pencil_copies:
        copy.start()
    pencil[block] = total[pl.ds(block * owned, owned)]
    for copy in pencil_copies:
        copy.wait()
    cells = blocks * owned * slab

    def combine(table_ref, pair, sign):
        both = dot_left(table_ref, pair)
        real = both[:cells, :lateral] + sign * both[cells:, lateral:]
        imag = both[:cells, lateral:] - sign * both[cells:, :lateral]
        return real, imag

    pair = dot_right(pencil[...].reshape(cells, lateral), ahead_y_ref)
    real, imag = combine(ahead_x_ref, pair, 1.0)
    pair = jnp.concatenate([real * scale, imag * scale], axis=1)
    real, imag = combine(back_x_ref, pair, -1.0)
    result = dot_right(jnp.concatenate([real, imag], axis=1), back_y_ref)
    filtered[...] = result.reshape(blocks, owned, slab, lateral)
    return_copies = exchange(
        return_sems,
        "block",
        blocks,
        block,
        lambda p: filtered.at[p],
        lambda m: returned.at[m],
    )
    for copy in return_copies:
        copy.start()
    returned[block] = filtered[block]
    for copy in return_copies:
        copy.wait()
    out_ref[...] = returned[...].reshape(kept, slab, lateral)


def run_steps(blocks, shots, fused, direct, stored, mass, out_dims):
    snap_steps, courant = direct[:2]
    slots, step_count = snap_steps.shape
    depth_cells, slab, lateral = courant.shape
    half = depth_cells // 2
    dma = pltpu.SemaphoreType.DMA
    cube = (depth_cells, slab, lateral)
    scratch = [pltpu.VMEM(array.shape, array.dtype) for array in stored]
    scratch += [
        dma((len(stored) + 1, slots)),
        pltpu.VMEM((2, slots) + cube, jnp.float32),
        pltpu.VMEM((2, slots, depth_cells * slab, lateral), jnp.bfloat16),
        pltpu.VMEM((2, slots, depth_cells * slab, lateral), jnp.bfloat16),
        pltpu.VMEM(cube, jnp.float32),
        pltpu.VMEM(cube, jnp.float32),
        pltpu.VMEM((step_count - 1, slots, 2, half, 8, lateral), jnp.float32),
        pltpu.VMEM((step_count - 1, slots, 2, half, 8, lateral), jnp.float32),
        dma((2, step_count - 1, slots, 2)),
    ]
    operands = list(direct) + list(stored)
    specs = [SM] + [VM] * (len(direct) - 1) + [pl.BlockSpec(memory_space=pltpu.HBM)] * len(stored)
    if fused:
        operands.append(mass)
        specs.append(VM)
        kept = depth_cells // shots
        owned = kept // blocks
        lanes = stored[4].shape[1]
        scratch += [
            pltpu.VMEM((mass.shape[0], lanes), jnp.float32),
            pltpu.VMEM((blocks, mass.shape[0], lanes), jnp.float32),
            pltpu.VMEM((shots, kept, slab, lateral), jnp.float32),
            pltpu.VMEM((kept, slab, lateral), jnp.float32),
            pltpu.VMEM((blocks, owned, slab, lateral), jnp.float32),
            pltpu.VMEM((blocks, owned, slab, lateral), jnp.float32),
            pltpu.VMEM((blocks, owned, slab, lateral), jnp.float32),
            dma((2, blocks)),
            dma((2, shots)),
            dma((2, blocks)),
            dma((2, blocks)),
        ]
    return pl.pallas_call(
        functools.partial(step_kernel, blocks, shots, fused, len(stored)),
        out_shape=jax.ShapeDtypeStruct(out_dims, jnp.float32),
        in_specs=specs,
        out_specs=VM,
        scratch_shapes=scratch,
        compiler_params=pltpu.CompilerParams(
            collective_id=0, has_side_effects=True, vmem_limit_bytes=58 * 2**20
        ),
    )(*operands)


def spectral_tail(gradient, mass_spectrum):
    summed = lax.psum_scatter(gradient, "shot", scatter_dimension=0, tiled=True)
    lateral = summed.shape[2]
    cos_y, sin_y = (jnp.asarray(v, jnp.float32) for v in fourier_np(lateral))
    real = jnp.einsum("zxy,yk->zkx", summed, cos_y, precision=FULL)
    imag = -jnp.einsum("zxy,yk->zkx", summed, sin_y, precision=FULL)
    pencils = lax.all_to_all(
        jnp.stack([real, imag]), "block", split_axis=2, concat_axis=3, tiled=True
    )
    across = pencils.shape[3]
    cos_x, sin_x = (jnp.asarray(v, jnp.float32) for v in fourier_np(across))

    def turn(real, imag, sign):
        first = jnp.einsum("zkx,xa->zka", real, cos_x, precision=FULL)
        first += sign * jnp.einsum("zkx,xa->zka", imag, sin_x, precision=FULL)
        second = jnp.einsum("zkx,xa->zka", imag, cos_x, precision=FULL)
        second -= sign * jnp.einsum("zkx,xa->zka", real, sin_x, precision=FULL)
        return first, second

    real, imag = turn(pencils[0], pencils[1], 1.0)
    real, imag = turn(real * mass_spectrum[None], imag * mass_spectrum[None], -1.0)
    back = lax.all_to_all(
        jnp.stack([real, imag]), "block", split_axis=3, concat_axis=2, tiled=True
    )
    spatial = jnp.einsum("zkx,ky->zxy", back[0], cos_y, precision=FULL)
    spatial -= jnp.einsum("zkx,ky->zxy", back[1], sin_y, precision=FULL)
    return spatial / float(across * lateral)


def per_device(
    courant, snapshots, residuals, receivers, sources, snap_steps, live_counts, mass_spectrum
):
    depth_cells, slab, lateral = courant.shape
    blocks = lax.axis_size("block")
    shots = lax.axis_size("shot")
    half = depth_cells // 2
    kept = depth_cells // shots
    fused = kept % blocks == 0

    injected, edges, fade = inject_all(
        jnp.transpose(receivers, (1, 0, 2)),
        jnp.transpose(residuals, (1, 0, 2)),
        sources,
        live_counts,
        depth_cells,
        slab,
        lateral,
    )
    lateral_table = difference_table(np.arange(lateral), np.arange(lateral))
    direct = [
        snap_steps,
        courant,
        jnp.asarray(plane_tables(half, slab), jnp.bfloat16),
        jnp.asarray(np.concatenate([lateral_table] * 2, axis=0), jnp.bfloat16),
    ]
    stored = [injected, edges, snapshots, fade]
    if not fused:
        dims = (depth_cells, slab, lateral)
        summed = run_steps(blocks, shots, False, direct, stored, None, dims)
        return spectral_tail(summed, mass_spectrum)

    owned = kept // blocks
    wide = blocks * slab
    cos_y, sin_y = fourier_np(lateral)
    cos_x, sin_x = fourier_np(wide)
    cells = owned * wide

    def ordered(table):
        grid = np.zeros((owned, wide, blocks, owned, slab))
        for z in range(owned):
            grid[z, :, :, z, :] = table.reshape(wide, blocks, slab)
        return grid.reshape(cells, cells)

    cos_ahead, sin_ahead = ordered(cos_x), ordered(sin_x)
    lanes = -(-wide // 128) * 128
    spread = np.zeros((owned, wide, lanes))
    for z in range(owned):
        spread[z, :, :wide] = np.eye(wide)
    spread = spread.reshape(cells, lanes) / float(wide * lateral)
    tables = [
        np.concatenate([cos_y, -sin_y], axis=1),
        np.concatenate([cos_y, -sin_y], axis=0),
        np.concatenate([cos_ahead, sin_ahead], axis=0),
        np.concatenate([cos_ahead.T, sin_ahead.T], axis=0),
    ]
    stored.append(jnp.asarray(spread, jnp.float32))
    stored += [jnp.asarray(two_parts(table)) for table in tables]
    return run_steps(
        blocks, shots, True, direct, stored, mass_spectrum, (kept, slab, lateral)
    )


def solution(mesh):
    in_specs = (
        P("chain", "block", None),
        P(("chain", "shot"), None, None, "block", None),
        P(("chain", "shot"), None, None),
        P(("chain", "shot"), None, None),
        P(("chain", "shot"), None),
        P(("chain", "shot"), None),
        P(("chain", "shot")),
        P(("chain", "block"), None),
    )
    out_specs = P(("chain", "shot"), "block", None)
    return jax.shard_map(
        per_device, mesh=mesh, in_specs=in_specs, out_specs=out_specs, check_vma=False
    )
```

```python
import functools
import math

import jax
import jax.numpy as jnp
import ml_dtypes
import numpy as np
from jax import lax
from jax.experimental import pallas as pl
from jax.experimental.pallas import tpu as pltpu
from jax.sharding import PartitionSpec as P

stencil_weights = (-205.0 / 72.0, 8.0 / 5.0, -1.0 / 5.0, 8.0 / 315.0, -1.0 / 560.0)
mute_radius = 6.0
MESH = pl.DeviceIdType.MESH
VM = pl.BlockSpec(memory_space=pltpu.VMEM)
SM = pl.BlockSpec(memory_space=pltpu.SMEM)
FULL = lax.Precision.HIGHEST


def two_parts(table):
    high = table.astype(ml_dtypes.bfloat16)
    return np.stack([high, (table - high.astype(np.float64)).astype(ml_dtypes.bfloat16)])


stencil_unit = 8.0 / 315.0
unit_weights = (None, 63.0, -63.0 / 8.0, 1.0, -9.0 / 128.0)
centre_units = 3.0 * stencil_weights[0] / stencil_unit


def difference_table(rows, columns):
    gap = np.abs(np.asarray(rows)[:, None] - np.asarray(columns)[None, :])
    table = np.zeros(gap.shape, np.float64)
    for k in range(1, 5):
        table[gap == k] = unit_weights[k]
    return table


def plane_tables(planes, slab):
    cells = np.arange(slab)
    ghost = np.concatenate([np.arange(-4, 0), np.arange(slab, slab + 4)])
    depth = np.arange(planes)
    own = np.kron(np.eye(planes), difference_table(cells, cells))
    own += np.kron(difference_table(depth, depth), np.eye(slab))
    sides = np.kron(np.eye(planes), difference_table(cells, ghost))
    tables = []
    for near in (np.arange(planes, planes + 4), np.arange(-4, 0)):
        reach = np.kron(difference_table(depth, near), np.eye(slab))
        spare = np.zeros((planes * slab, 4 * slab))
        one = np.concatenate([own, sides, reach, spare], axis=1)
        tables.append(np.concatenate([one, one], axis=1))
    return np.stack(tables)


def fourier_np(length):
    counting = np.arange(length)
    angle = (counting[:, None] * counting[None, :] % length) * (2.0 * math.pi / length)
    return np.cos(angle), np.sin(angle)


NT = (((1,), (1,)), ((), ()))
GROUP = 128


def inject_kernel(
    slab,
    own_size,
    edge_size,
    receivers_ref,
    residuals_ref,
    sources_ref,
    live_ref,
    tri_ref,
    out_ref,
    ghost_ref,
    fade_ref,
    marks,
    facts,
    ranks,
):
    s = pl.program_id(0)
    start = lax.axis_index("block") * slab
    steps = residuals_ref.shape[0]
    count = receivers_ref.shape[2]
    chunks = count // GROUP
    rows, lateral = out_ref.shape[2:]
    ghost_rows = ghost_ref.shape[1]
    depth_cells = rows // slab

    live = jnp.where(s < live_ref[0], 1.0, 0.0)
    scale = 1.0 / (mute_radius * mute_radius)
    place = [sources_ref[s, i].astype(jnp.float32) for i in range(3)]
    flat = (slab, lateral)
    across = (lax.broadcasted_iota(jnp.int32, flat, 0) + start).astype(jnp.float32) - place[1]
    side = lax.broadcasted_iota(jnp.int32, flat, 1).astype(jnp.float32) - place[2]
    fade_flat = live * jnp.exp(-(across * across + side * side) * scale)
    gap = lax.broadcasted_iota(jnp.int32, (depth_cells, lateral), 0).astype(jnp.float32) - place[0]
    fade_depth = jnp.exp(-(gap * gap) * scale)
    for z in range(depth_cells):
        fade_ref[0, z] = live - fade_depth[z : z + 1] * fade_flat

    depth = receivers_ref[0, pl.ds(s, 1), :]
    local = receivers_ref[1, pl.ds(s, 1), :] - start
    lateral_pos = receivers_ref[2, pl.ds(s, 1), :]
    facts[0:1, :] = depth.astype(jnp.float32)
    facts[2:3, :] = (lateral_pos // 16).astype(jnp.float32)
    facts[3:4, :] = lax.rem(lateral_pos, 16).astype(jnp.float32)
    for t in range(steps):
        value = residuals_ref[t, pl.ds(s, 1), :]
        high = value.astype(jnp.bfloat16).astype(jnp.float32)
        facts[4 + 2 * t : 5 + 2 * t, :] = high
        facts[5 + 2 * t : 6 + 2 * t, :] = value - high
    used = 4 + 2 * steps
    facts[used:, :] = jnp.zeros((facts.shape[0] - used, count), jnp.float32)

    def rank(inside):
        flag = jnp.where(inside, 1.0, 0.0)
        for c in range(chunks):
            marks[c : c + 1, :] = flag[:, c * GROUP : (c + 1) * GROUP]
        mark = marks[...]
        through = jnp.dot(
            mark.astype(jnp.bfloat16), tri_ref[...], preferred_element_type=jnp.float32
        )
        total = jnp.zeros((1, 1), jnp.float32)
        for c in range(chunks):
            ranks[c : c + 1, :] = jnp.where(
                mark[c : c + 1] > 0.0, through[c : c + 1] + (total - 1.0), -1.0
            ).astype(jnp.int32)
            total = total + through[c : c + 1, GROUP - 1 :]
        return jnp.sum(flag).astype(jnp.int32)

    def gather(first, size):
        slot = lax.broadcasted_iota(jnp.int32, (size, GROUP), 0) + first
        pick = jnp.concatenate(
            [
                jnp.where(slot == ranks[c : c + 1, :], 1.0, 0.0).astype(jnp.bfloat16)
                for c in range(chunks)
            ],
            axis=1,
        )
        return lax.dot_general(
            facts[...].astype(jnp.bfloat16), pick, NT, preferred_element_type=jnp.float32
        )

    def spread(found, width, row_count, t_list):
        where = found[0:1] * float(width) + found[1:2]
        size = found.shape[1]
        row = lax.broadcasted_iota(jnp.int32, (row_count, size), 0)
        row = jnp.where(row == where.astype(jnp.int32), 1.0, 0.0).astype(jnp.bfloat16)
        row = jnp.concatenate([row, row], axis=1)
        lane = (found[2:3] * 16.0 + found[3:4]).astype(jnp.int32)
        hit = lax.broadcasted_iota(jnp.int32, (lateral, size), 0) == lane
        for t in t_list:
            pair = jnp.concatenate(
                [
                    jnp.where(hit, found[4 + 2 * t + i : 5 + 2 * t + i], 0.0).astype(jnp.bfloat16)
                    for i in range(2)
                ],
                axis=1,
            )
            yield t, lax.dot_general(row, pair, NT, preferred_element_type=jnp.float32)

    inside = (local >= 0) & (local < slab)
    facts[1:2, :] = jnp.where(inside, local, 0).astype(jnp.float32)
    own_total = rank(inside)
    for t, value in spread(gather(0, own_size), slab, rows, range(steps)):
        out_ref[0, t] = value

    def own_group(group, carry):
        for t, add in spread(gather(own_size + group * GROUP, GROUP), slab, rows, range(steps)):
            out_ref[0, t] += add
        return carry

    lax.fori_loop(0, jnp.maximum(own_total - own_size + GROUP - 1, 0) // GROUP, own_group, 0)

    left = (local >= -4) & (local < 0)
    right = (local >= slab) & (local < slab + 4)
    column = jnp.where(left, local + 4, jnp.where(right, local - slab + 4, 0))
    facts[1:2, :] = column.astype(jnp.float32)
    edge_total = rank(left | right)
    for _, value in spread(gather(0, edge_size), 8, ghost_rows, (0,)):
        ghost_ref[0] = value

    def ghost_group(group, carry):
        for _, add in spread(gather(edge_size + group * GROUP, GROUP), 8, ghost_rows, (0,)):
            ghost_ref[0] += add
        return carry

    lax.fori_loop(0, jnp.maximum(edge_total - edge_size + GROUP - 1, 0) // GROUP, ghost_group, 0)


def inject_all(receivers, residuals, sources, live_counts, depth_cells, slab, lateral):
    steps, slots, count = residuals.shape
    rows = depth_cells * slab
    ghost_rows = depth_cells * 8
    blocks = lax.axis_size("block")
    own_size = min(count, (-(-count // blocks // GROUP) + 1) * GROUP)
    edge_size = min(count, (-(-8 * count // (blocks * slab) // GROUP) + 1) * GROUP)
    tri = jnp.asarray(np.triu(np.ones((GROUP, GROUP))), jnp.bfloat16)
    fact_rows = -(-(4 + 2 * steps) // 16) * 16
    return pl.pallas_call(
        functools.partial(inject_kernel, slab, own_size, edge_size),
        grid=(slots,),
        in_specs=[VM, VM, SM, SM, VM],
        out_specs=[
            pl.BlockSpec((1, steps, rows, lateral), lambda s: (s, 0, 0, 0)),
            pl.BlockSpec((1, ghost_rows, lateral), lambda s: (s, 0, 0)),
            pl.BlockSpec((1, depth_cells, slab, lateral), lambda s: (s, 0, 0, 0)),
        ],
        out_shape=[
            jax.ShapeDtypeStruct((slots, steps, rows, lateral), jnp.float32),
            jax.ShapeDtypeStruct((slots, ghost_rows, lateral), jnp.float32),
            jax.ShapeDtypeStruct((slots, depth_cells, slab, lateral), jnp.float32),
        ],
        scratch_shapes=[
            pltpu.VMEM((count // GROUP, GROUP), jnp.float32),
            pltpu.VMEM((fact_rows, count), jnp.float32),
            pltpu.VMEM((count // GROUP, GROUP), jnp.int32),
        ],
        compiler_params=pltpu.CompilerParams(vmem_limit_bytes=62 * 2**20),
    )(receivers, residuals, sources, live_counts, tri)


def split_value(value):
    high = value.astype(jnp.bfloat16)
    low = (value - high.astype(jnp.float32)).astype(jnp.bfloat16)
    return high, low


def dot(left, right):
    return jnp.dot(left, right, preferred_element_type=jnp.float32)


def dot_right(value, table_ref):
    high, low = split_value(value)
    return dot(high, table_ref[0]) + (dot(low, table_ref[0]) + dot(high, table_ref[1]))


def dot_left(table_ref, value):
    high, low = split_value(value)
    return dot(table_ref[0], high) + (dot(table_ref[0], low) + dot(table_ref[1], high))


def step_kernel(blocks, shots, fused, late, *refs):
    steps_ref, courant_ref, plane_ref, lateral_ref, *rest = refs
    stored = rest[:late]
    if fused:
        mass_ref = rest[late]
        rest = rest[1:]
    out_ref, *rest = rest[late:]
    local = rest[:late]
    (load_sems, field, highs, lows, scaled, gradient, ghost, outgoing, ghost_sems, *rest) = rest[
        late:
    ]
    inj_ref, edge_ref, snaps_ref, fade_ref = local[:4]
    slots, step_count = steps_ref.shape
    depth_cells, slab, lateral = courant_ref.shape
    half = depth_cells // 2
    block = lax.axis_index("block")
    shot = lax.axis_index("shot")

    def load(i, s):
        if i == 0:
            span = (s, slice(0, 2))
            return pltpu.make_async_copy(stored[0].at[span], local[0].at[span], load_sems.at[0, s])
        return pltpu.make_async_copy(stored[i].at[s], local[i].at[s], load_sems.at[i, s])

    def load_later(s):
        span = (s, slice(2, steps_ref.shape[1] + 1))
        return pltpu.make_async_copy(stored[0].at[span], local[0].at[span], load_sems.at[late, s])

    def load_table(i):
        return pltpu.make_async_copy(stored[i], local[i], load_sems.at[i, 0])

    for s in range(slots):
        load(2, s).start()
    for s in range(slots):
        for i in (0, 1, 3):
            load(i, s).start()
    for s in range(slots):
        load_later(s).start()
    for i in range(4, late):
        load_table(i).start()

    barrier = pltpu.get_barrier_semaphore()

    @pl.when(block > 0)
    def _():
        pl.semaphore_signal(barrier, inc=1, device_id={"block": block - 1}, device_id_type=MESH)

    @pl.when(block < blocks - 1)
    def _():
        pl.semaphore_signal(barrier, inc=1, device_id={"block": block + 1}, device_id_type=MESH)

    if fused:
        (
            mass_own,
            mass_all,
            parts,
            total,
            pencil,
            filtered,
            returned,
            mass_sems,
            part_sems,
            pencil_sems,
            return_sems,
        ) = rest
        for off in range(1, blocks):
            peer = lax.rem(block + off, blocks)

            @pl.when((peer != block - 1) & (peer != block + 1))
            def _(peer=peer):
                pl.semaphore_signal(barrier, inc=1, device_id={"block": peer}, device_id_type=MESH)

        for off in range(1, shots):
            peer = lax.rem(shot + off, shots)
            pl.semaphore_signal(barrier, inc=1, device_id={"shot": peer}, device_id_type=MESH)
        mass_own[...] = jnp.zeros_like(mass_own)
        mass_own[:, 0 : mass_ref.shape[1]] = mass_ref[...]
    gradient[...] = jnp.zeros_like(gradient)
    scaled[...] = courant_ref[...] * stencil_unit

    @pl.when(block == 0)
    def _():
        ghost[:, :, 0] = jnp.zeros((step_count - 1, slots, half, 8, lateral), jnp.float32)

    @pl.when(block == blocks - 1)
    def _():
        ghost[:, :, 1] = jnp.zeros((step_count - 1, slots, half, 8, lateral), jnp.float32)

    if fused:
        pl.semaphore_wait(barrier, blocks - 1 + shots - 1)
    else:

        @pl.when(block > 0)
        def _():
            pl.semaphore_wait(barrier, 1)

        @pl.when(block < blocks - 1)
        def _():
            pl.semaphore_wait(barrier, 1)

    def exchange(sems, axis, size, me, src, dst):
        copies = []
        for off in range(1, size):
            peer = lax.rem(me + off, size)
            copies.append(
                pltpu.make_async_remote_copy(
                    src_ref=src(peer),
                    dst_ref=dst(me),
                    send_sem=sems.at[0, off],
                    recv_sem=sems.at[1, off],
                    device_id={axis: peer},
                    device_id_type=MESH,
                )
            )
        return copies

    if fused:
        mass_copies = exchange(
            mass_sems, "block", blocks, block, lambda p: mass_own, lambda m: mass_all.at[m]
        )
        for copy in mass_copies:
            copy.start()
        mass_all[block] = mass_own[...]

    def to_left(t, s):
        return pltpu.make_async_remote_copy(
            src_ref=outgoing.at[t, s, 0],
            dst_ref=ghost.at[t, s, 1],
            send_sem=ghost_sems.at[0, t, s, 0],
            recv_sem=ghost_sems.at[1, t, s, 1],
            device_id={"block": lax.rem(block + blocks - 1, blocks)},
            device_id_type=MESH,
        )

    def to_right(t, s):
        return pltpu.make_async_remote_copy(
            src_ref=outgoing.at[t, s, 1],
            dst_ref=ghost.at[t, s, 0],
            send_sem=ghost_sems.at[0, t, s, 1],
            recv_sem=ghost_sems.at[1, t, s, 0],
            device_id={"block": lax.rem(block + 1, blocks)},
            device_id_type=MESH,
        )

    lower = lax.broadcasted_iota(jnp.int32, (half, 8, lateral), 1) < 4

    def swap(value):
        return jnp.concatenate([value[:, 4:8], value[:, 0:4]], axis=1)

    def send_faces(t, s, plane):
        first = field[plane, s, 0:half, 0:8, :]
        second = field[plane, s, half:depth_cells, 0:8, :]
        outgoing[t, s, 0] = jnp.where(lower, first, swap(second))
        first = field[plane, s, 0:half, slab - 8 : slab, :]
        second = field[plane, s, half:depth_cells, slab - 8 : slab, :]
        outgoing[t, s, 1] = jnp.where(lower, swap(first), second)

        @pl.when(block > 0)
        def _():
            to_left(t, s).start()

        @pl.when(block < blocks - 1)
        def _():
            to_right(t, s).start()

    spare = jnp.zeros((4 * slab, lateral), jnp.bfloat16)
    rows = half * slab

    def bend(t, s, c, tile):
        now = t % 2
        near = slice(rows, rows + 4 * slab) if c == 0 else slice(rows - 4 * slab, rows)
        here = slice(c * rows, (c + 1) * rows)
        stack = []
        if t == 0:
            own = split_value(inj_ref[s, 0, here])
            reach = split_value(inj_ref[s, 0, near])
        else:
            own = (highs[now, s, here], lows[now, s, here])
            reach = (highs[now, s, near], lows[now, s, near])
        side = split_value(tile)
        for i in range(2):
            stack += [own[i], side[i], reach[i], spare]
        result = dot(plane_ref[c], jnp.concatenate(stack, axis=0))
        return result + dot(jnp.concatenate(own, axis=1), lateral_ref[...])

    def update(t, s, c, sums):
        now, later = t % 2, (t + 1) % 2
        chosen = steps_ref[s, t]
        for z in range(half):
            depth = c * half + z
            span = slice(depth * slab, (depth + 1) * slab)
            centre = inj_ref[s, 0, span] if t == 0 else field[now, s, depth]
            fresh = 2.0 * centre + inj_ref[s, t + 1, span]
            if t == 1:
                fresh -= inj_ref[s, 0, span]
            elif t > 1:
                fresh -= field[later, s, depth]
            fresh += scaled[depth] * (sums[z * slab : (z + 1) * slab] + centre_units * centre)
            if t < step_count - 1:
                field[later, s, depth] = fresh
                highs[later, s, span], lows[later, s, span] = split_value(fresh)
            shown = snaps_ref[s, chosen, depth].astype(jnp.float32)
            gradient[depth] += fade_ref[s, depth] * (fresh * shown)

    def tiles(t, s):
        if t == 0:
            return [edge_ref[s, c * half * 8 : (c + 1) * half * 8] for c in range(2)]

        from_left = ghost[t - 1, s, 0]
        from_right = ghost[t - 1, s, 1]
        return [
            jnp.where(lower, from_left, swap(from_right)).reshape(half * 8, lateral),
            jnp.where(lower, swap(from_left), from_right).reshape(half * 8, lateral),
        ]

    def arrive(t, s):
        if t == 0:
            for i in (0, 1, 3):
                load(i, s).wait()
            return
        if t == 1:
            load_later(s).wait()

        @pl.when(block > 0)
        def _():
            to_right(t - 1, s).wait_recv()

        @pl.when(block < blocks - 1)
        def _():
            to_left(t - 1, s).wait_recv()

    for s in range(slots):
        load(2, s).wait()

    for t in range(step_count - 1):

        def advance(s, carry, t=t):
            arrive(t, s)
            tile = tiles(t, s)
            sums = [bend(t, s, c, tile[c]) for c in range(2)]
            for c in range(2):
                update(t, s, c, sums[c])
            send_faces(t, s, (t + 1) % 2)
            return carry

        lax.fori_loop(0, slots, advance, 0)

    if fused:
        kept = depth_cells // shots
        owned = kept // blocks
        part_copies = exchange(
            part_sems,
            "shot",
            shots,
            shot,
            lambda p: gradient.at[pl.ds(p * kept, kept)],
            lambda m: parts.at[m],
        )
    t = step_count - 1
    for c in range(2):

        def finish(s, carry, c=c):
            if c == 0:
                arrive(t, s)
            update(t, s, c, bend(t, s, c, tiles(t, s)[c]))
            return carry

        lax.fori_loop(0, slots, finish, 0)
        if fused:
            for off in range(1, shots):
                peer = lax.rem(shot + off, shots)

                @pl.when((peer * kept >= c * half) & (peer * kept < (c + 1) * half))
                def _(off=off):
                    part_copies[off - 1].start()

    def drain(index, carry):
        t = index // slots
        s = lax.rem(index, slots)

        @pl.when(block > 0)
        def _():
            to_left(t, s).wait_send()

        @pl.when(block < blocks - 1)
        def _():
            to_right(t, s).wait_send()

        return carry

    lax.fori_loop(0, (step_count - 1) * slots, drain, 0)
    if not fused:
        out_ref[...] = gradient[...]
        return

    for i in range(4, late):
        load_table(i).wait()
    spread_ref, ahead_y_ref, back_y_ref, ahead_x_ref, back_x_ref = local[4:]
    parts[shot] = gradient[pl.ds(shot * kept, kept)]
    for copy in mass_copies:
        copy.wait()
    wide = mass_all[...].reshape(lateral, mass_all.shape[2])
    scale = lax.dot_general(
        spread_ref[...], wide, NT, preferred_element_type=jnp.float32, precision=FULL
    )
    for copy in part_copies:
        copy.wait()
    summed = parts[0]
    for i in range(1, shots):
        summed = summed + parts[i]
    total[...] = summed
    pencil_copies = exchange(
        pencil_sems,
        "block",
        blocks,
        block,
        lambda p: total.at[pl.ds(p * owned, owned)],
        lambda m: pencil.at[m],
    )
    for copy in pencil_copies:
        copy.start()
    pencil[block] = total[pl.ds(block * owned, owned)]
    for copy in pencil_copies:
        copy.wait()
    cells = blocks * owned * slab

    def combine(table_ref, pair, sign):
        both = dot_left(table_ref, pair)
        real = both[:cells, :lateral] + sign * both[cells:, lateral:]
        imag = both[:cells, lateral:] - sign * both[cells:, :lateral]
        return real, imag

    pair = dot_right(pencil[...].reshape(cells, lateral), ahead_y_ref)
    real, imag = combine(ahead_x_ref, pair, 1.0)
    pair = jnp.concatenate([real * scale, imag * scale], axis=1)
    real, imag = combine(back_x_ref, pair, -1.0)
    result = dot_right(jnp.concatenate([real, imag], axis=1), back_y_ref)
    filtered[...] = result.reshape(blocks, owned, slab, lateral)
    return_copies = exchange(
        return_sems,
        "block",
        blocks,
        block,
        lambda p: filtered.at[p],
        lambda m: returned.at[m],
    )
    for copy in return_copies:
        copy.start()
    returned[block] = filtered[block]
    for copy in return_copies:
        copy.wait()
    out_ref[...] = returned[...].reshape(kept, slab, lateral)


def run_steps(blocks, shots, fused, direct, stored, mass, out_dims):
    snap_steps, courant = direct[:2]
    slots, step_count = snap_steps.shape
    depth_cells, slab, lateral = courant.shape
    half = depth_cells // 2
    dma = pltpu.SemaphoreType.DMA
    cube = (depth_cells, slab, lateral)
    scratch = [pltpu.VMEM(array.shape, array.dtype) for array in stored]
    scratch += [
        dma((len(stored) + 1, slots)),
        pltpu.VMEM((2, slots) + cube, jnp.float32),
        pltpu.VMEM((2, slots, depth_cells * slab, lateral), jnp.bfloat16),
        pltpu.VMEM((2, slots, depth_cells * slab, lateral), jnp.bfloat16),
        pltpu.VMEM(cube, jnp.float32),
        pltpu.VMEM(cube, jnp.float32),
        pltpu.VMEM((step_count - 1, slots, 2, half, 8, lateral), jnp.float32),
        pltpu.VMEM((step_count - 1, slots, 2, half, 8, lateral), jnp.float32),
        dma((2, step_count - 1, slots, 2)),
    ]
    operands = list(direct) + list(stored)
    specs = [SM] + [VM] * (len(direct) - 1) + [pl.BlockSpec(memory_space=pltpu.HBM)] * len(stored)
    if fused:
        operands.append(mass)
        specs.append(VM)
        kept = depth_cells // shots
        owned = kept // blocks
        lanes = stored[4].shape[1]
        scratch += [
            pltpu.VMEM((mass.shape[0], lanes), jnp.float32),
            pltpu.VMEM((blocks, mass.shape[0], lanes), jnp.float32),
            pltpu.VMEM((shots, kept, slab, lateral), jnp.float32),
            pltpu.VMEM((kept, slab, lateral), jnp.float32),
            pltpu.VMEM((blocks, owned, slab, lateral), jnp.float32),
            pltpu.VMEM((blocks, owned, slab, lateral), jnp.float32),
            pltpu.VMEM((blocks, owned, slab, lateral), jnp.float32),
            dma((2, blocks)),
            dma((2, shots)),
            dma((2, blocks)),
            dma((2, blocks)),
        ]
    return pl.pallas_call(
        functools.partial(step_kernel, blocks, shots, fused, len(stored)),
        out_shape=jax.ShapeDtypeStruct(out_dims, jnp.float32),
        in_specs=specs,
        out_specs=VM,
        scratch_shapes=scratch,
        compiler_params=pltpu.CompilerParams(
            collective_id=0, has_side_effects=True, vmem_limit_bytes=58 * 2**20
        ),
    )(*operands)


def spectral_tail(gradient, mass_spectrum):
    summed = lax.psum_scatter(gradient, "shot", scatter_dimension=0, tiled=True)
    lateral = summed.shape[2]
    cos_y, sin_y = (jnp.asarray(v, jnp.float32) for v in fourier_np(lateral))
    real = jnp.einsum("zxy,yk->zkx", summed, cos_y, precision=FULL)
    imag = -jnp.einsum("zxy,yk->zkx", summed, sin_y, precision=FULL)
    pencils = lax.all_to_all(
        jnp.stack([real, imag]), "block", split_axis=2, concat_axis=3, tiled=True
    )
    across = pencils.shape[3]
    cos_x, sin_x = (jnp.asarray(v, jnp.float32) for v in fourier_np(across))

    def turn(real, imag, sign):
        first = jnp.einsum("zkx,xa->zka", real, cos_x, precision=FULL)
        first += sign * jnp.einsum("zkx,xa->zka", imag, sin_x, precision=FULL)
        second = jnp.einsum("zkx,xa->zka", imag, cos_x, precision=FULL)
        second -= sign * jnp.einsum("zkx,xa->zka", real, sin_x, precision=FULL)
        return first, second

    real, imag = turn(pencils[0], pencils[1], 1.0)
    real, imag = turn(real * mass_spectrum[None], imag * mass_spectrum[None], -1.0)
    back = lax.all_to_all(
        jnp.stack([real, imag]), "block", split_axis=3, concat_axis=2, tiled=True
    )
    spatial = jnp.einsum("zkx,ky->zxy", back[0], cos_y, precision=FULL)
    spatial -= jnp.einsum("zkx,ky->zxy", back[1], sin_y, precision=FULL)
    return spatial / float(across * lateral)


def per_device(
    courant, snapshots, residuals, receivers, sources, snap_steps, live_counts, mass_spectrum
):
    depth_cells, slab, lateral = courant.shape
    blocks = lax.axis_size("block")
    shots = lax.axis_size("shot")
    half = depth_cells // 2
    kept = depth_cells // shots
    fused = kept % blocks == 0

    injected, edges, fade = inject_all(
        jnp.transpose(receivers, (1, 0, 2)),
        jnp.transpose(residuals, (1, 0, 2)),
        sources,
        live_counts,
        depth_cells,
        slab,
        lateral,
    )
    lateral_table = difference_table(np.arange(lateral), np.arange(lateral))
    direct = [
        snap_steps,
        courant,
        jnp.asarray(plane_tables(half, slab), jnp.bfloat16),
        jnp.asarray(np.concatenate([lateral_table] * 2, axis=0), jnp.bfloat16),
    ]
    stored = [injected, edges, snapshots, fade]
    if not fused:
        dims = (depth_cells, slab, lateral)
        summed = run_steps(blocks, shots, False, direct, stored, None, dims)
        return spectral_tail(summed, mass_spectrum)

    owned = kept // blocks
    wide = blocks * slab
    cos_y, sin_y = fourier_np(lateral)
    cos_x, sin_x = fourier_np(wide)
    cells = owned * wide

    def ordered(table):
        grid = np.zeros((owned, wide, blocks, owned, slab))
        for z in range(owned):
            grid[z, :, :, z, :] = table.reshape(wide, blocks, slab)
        return grid.reshape(cells, cells)

    cos_ahead, sin_ahead = ordered(cos_x), ordered(sin_x)
    lanes = -(-wide // 128) * 128
    spread = np.zeros((owned, wide, lanes))
    for z in range(owned):
        spread[z, :, :wide] = np.eye(wide)
    spread = spread.reshape(cells, lanes) / float(wide * lateral)
    tables = [
        np.concatenate([cos_y, -sin_y], axis=1),
        np.concatenate([cos_y, -sin_y], axis=0),
        np.concatenate([cos_ahead, sin_ahead], axis=0),
        np.concatenate([cos_ahead.T, sin_ahead.T], axis=0),
    ]
    stored.append(jnp.asarray(spread, jnp.float32))
    stored += [jnp.asarray(two_parts(table)) for table in tables]
    return run_steps(
        blocks, shots, True, direct, stored, mass_spectrum, (kept, slab, lateral)
    )


def solution(mesh):
    in_specs = (
        P("chain", "block", None),
        P(("chain", "shot"), None, None, "block", None),
        P(("chain", "shot"), None, None),
        P(("chain", "shot"), None, None),
        P(("chain", "shot"), None),
        P(("chain", "shot"), None),
        P(("chain", "shot")),
        P(("chain", "block"), None),
    )
    out_specs = P(("chain", "shot"), "block", None)
    return jax.shard_map(
        per_device, mesh=mesh, in_specs=in_specs, out_specs=out_specs, check_vma=False
    )
```
